128 devices in a mesh: dp: 16 (over y, z), tensor: 8 (over x, core).
Axes of the slice: x: 4, y: 4, z: 4, core: 2. Of those that a mesh axis runs over, the one named last changes fastest.
Arguments:
- hidden_in: bfloat16 [9216, 8192], P(('dp', 'tensor')), may hold values from -600 to 600
- norm_gain: float32 [8192], replicated, may hold values from 0.1 to 1.9
- query_weight: bfloat16 [8192, 4096], P('dp', 'tensor'), may hold values from -0.0625 to 0.0625
- keyval_weight: bfloat16 [8192, 2, 1024], P('dp', None, 'tensor'), may hold values from -0.0625 to 0.0625
- query_bias: float32 [4096], P('tensor'), may hold values from -40 to 40
- keyval_bias: float32 [2, 1024], P(None, 'tensor'), may hold values from -40 to 40
- out_weight: bfloat16 [4096, 8192], P('tensor', 'dp'), may hold values from -0.09375 to 0.09375
- bundle_row_lengths: int32 [16], replicated, may hold values from 1 to 72, as said below
- move_plan: int32 [16], replicated, may hold values from 0 to 15, each once
- first_len: int32 [16, 16], replicated, may hold values from 1 to 72, as said below
Outputs:
- attended: bfloat16 [9216, 8192], P(('dp', 'tensor'))
The draws below stay inside these ranges and needn't reach their ends.
Inputs may be any that keep to these rules, and one draw needn't show every extreme that they name: `bundle_row_lengths`: the lengths sum to 576; exactly one of them is 72. `move_plan`: each value appears once. first_len[h, b] is at least 1 and at most bundle_row_lengths[b].
All inputs are finite; a program needn't handle non-finite values.
Results may differ from the reference program's by a relative error of at most 0.024.
Values may be sent and summed in bfloat16 or wider, within the bound.
No kernel may reach another device: no remote copies, remote signals or barrier semaphores. Data moves between devices by JAX's collectives and lax.ppermute only.
A program may use at most 128 MiB of HBM per device.

```python
import math
import jax
import jax.numpy as jnp
from jax import lax

D = 8192
HEADS = 32
KV = 8
HD = 128
TOK_GRP = 576
TOKENS = 9216
BUNDLE_COUNT = 16
BUNDLE_MOST = 72
N_DP = 16
N_TENSOR = 8


def bundle_sizes(key):
    remaining = TOK_GRP - BUNDLE_MOST
    base_length = remaining // (BUNDLE_COUNT - 1)
    remainder_rows = remaining - base_length * (BUNDLE_COUNT - 1)
    random_share = jax.random.randint(jax.random.fold_in(key, 101), (BUNDLE_COUNT - 1,), 0, base_length, dtype=jnp.int32)
    extra_rows = (jnp.arange(BUNDLE_COUNT - 1, dtype=jnp.int32) < remainder_rows).astype(jnp.int32)
    other_bundles = (base_length + extra_rows + random_share - jnp.roll(random_share, -1)).astype(jnp.int32)
    all_sizes = jnp.concatenate([jnp.full((1,), BUNDLE_MOST, jnp.int32), other_bundles])
    return jax.random.permutation(jax.random.fold_in(key, 102), all_sizes)


def draw_bundle_row_lengths(key, part):
    drawn_sizes = bundle_sizes(key)
    return drawn_sizes


def draw_first_len(key, part):
    drawn_sizes = bundle_sizes(key)
    key = jax.random.fold_in(key, 2)
    drawn = jax.random.randint(key, (BUNDLE_COUNT, BUNDLE_COUNT), 1, drawn_sizes[None, :] + 1, dtype=jnp.int32)
    pack_ids = jnp.arange(BUNDLE_COUNT, dtype=jnp.int32)[:, None]
    longest = (drawn_sizes == BUNDLE_MOST)[None, :]
    drawn = jnp.where(longest & (pack_ids == 0), BUNDLE_MOST, drawn)
    drawn = jnp.where(longest & (pack_ids == 1), 1, drawn)
    return drawn.astype(jnp.int32)


def draw_hidden_in(key, part):
    key = jax.random.fold_in(key, 3)
    noise_key, row_key, column_key = jax.random.split(key, 3)
    column_scale = jnp.exp(jax.random.uniform(column_key, (1, D), jnp.float32, 0.0, math.log(10.0)))
    row_scale = jnp.exp(jax.random.uniform(row_key, (TOKENS, 1), jnp.float32, 0.0, math.log(10.0)))
    values = jnp.clip(jax.random.normal(noise_key, (TOKENS, D), jnp.float32), -6.0, 6.0)
    return (values * row_scale * column_scale).astype(jnp.bfloat16)


def draw_query_bias(key, part):
    key = jax.random.fold_in(key, 4)
    return jnp.clip(jax.random.normal(key, (HEADS * HD,), jnp.float32), -5.0, 5.0)


def draw_keyval_bias(key, part):
    key = jax.random.fold_in(key, 5)
    value_part = jnp.clip(jax.random.normal(key, (1, KV * HD), jnp.float32), -5.0, 5.0)
    key_part = jnp.clip(jax.random.normal(jax.random.fold_in(key, 6), (1, KV * HD), jnp.float32), -5.0, 5.0)
    return jnp.concatenate([key_part, value_part], axis=0)


def levels(key, extent, cuts, low, high):
    def one(dim, blocks):
        heights = jax.random.uniform(jax.random.fold_in(jax.random.fold_in(key, 6), dim), (blocks,), jnp.float32, low / len(cuts), high / len(cuts))
        return jnp.repeat(jnp.exp(heights), extent[dim] // blocks).reshape((-1,) + (1,) * (len(extent) - dim - 1))

    factor_of = one(*cuts[0])
    for cut in cuts[1:]:
        factor_of = factor_of * one(*cut)
    return factor_of


def bell_draw(stream_key, extent, spread, limit, shards=(), kind=jnp.bfloat16):
    result = jax.random.normal(stream_key, extent, jnp.float32) * spread
    if len(shards) > 0:
        result = levels(stream_key, extent, shards, -0.22, 0.18) * result
    return jnp.clip(result, min=-limit, max=limit).astype(kind)


def setup_inputs(seed: int = 0) -> dict:
    seeds = jax.random.split(jax.random.key(seed), 11)
    hidden_in = draw_hidden_in(jax.random.fold_in(seeds[10], 71), 0)
    norm_gain = jnp.clip(1.0 + 0.18 * jax.random.normal(seeds[1], (D,), jnp.float32), 0.1, 1.9)
    query_weight = bell_draw(seeds[2], (D, HEADS * HD), D ** -0.5, 0.0625, ((0, 16), (1, 8)))
    keyval_weight = bell_draw(seeds[3], (D, 2, KV * HD), D ** -0.5, 0.0625, ((0, 16), (2, 8)))
    query_bias = draw_query_bias(jax.random.fold_in(seeds[10], 71), 0)
    keyval_bias = draw_keyval_bias(jax.random.fold_in(seeds[10], 71), 0)
    out_weight = bell_draw(seeds[6], (HEADS * HD, D), (HEADS * HD) ** -0.5, 0.09375, ((0, 8), (1, 16)))
    bundle_row_lengths = draw_bundle_row_lengths(jax.random.fold_in(seeds[10], 71), 0)
    move_plan = jax.random.permutation(seeds[8], BUNDLE_COUNT).astype(jnp.int32)
    first_len = draw_first_len(jax.random.fold_in(seeds[10], 71), 0)
    return dict(hidden_in=hidden_in, norm_gain=norm_gain, query_weight=query_weight, keyval_weight=keyval_weight, query_bias=query_bias, keyval_bias=keyval_bias, out_weight=out_weight, bundle_row_lengths=bundle_row_lengths, move_plan=move_plan, first_len=first_len)


THETA = 1000000.0
EPS = 1e-06

def rotate_heads(values, places):
    half_dim = values.shape[-1] // 2
    indices = jnp.arange(half_dim, dtype=jnp.float32)
    frequency = THETA ** (-2.0 * indices / values.shape[-1])
    angles = places[:, None] * frequency[None, :]
    cosines = jnp.cos(angles)[:, None, :]
    sine_vals = jnp.sin(angles)[:, None, :]
    lower_half = values[..., :half_dim]
    upper_half = values[..., half_dim:]
    return jnp.concatenate([lower_half * cosines - upper_half * sine_vals, upper_half * cosines + lower_half * sine_vals], axis=-1)

def document_layout(bundle_row_lengths, first_row, row_count):
    offsets = (jnp.cumsum(bundle_row_lengths) - bundle_row_lengths).astype(jnp.int32)
    places = jnp.arange(row_count, dtype=jnp.int32)
    bundle_id = (lax.optimization_barrier(jnp.sum((places[:, None] >= offsets[None, :]).astype(jnp.int32), axis=1)) - 1).astype(jnp.int32)
    selector = (bundle_id[:, None] == jnp.arange(offsets.shape[0], dtype=jnp.int32)[None, :]).astype(jnp.int32)
    starts = lax.optimization_barrier(jnp.sum(selector * offsets[None, :], axis=1)).astype(jnp.int32)
    splits = lax.optimization_barrier(jnp.sum(selector * first_row[None, :], axis=1)).astype(jnp.int32)
    second = (places - starts >= splits).astype(jnp.int32)
    segment = (bundle_id * 2 + second).astype(jnp.int32)
    doc_start = starts + second * splits
    return (segment, (places - doc_start).astype(jnp.float32), starts, bundle_id)

def normalize(rows, norm_gain):
    values = rows.astype(jnp.float32)
    scale = lax.rsqrt(lax.optimization_barrier(jnp.mean(values * values, axis=1, keepdims=True)) + EPS)
    return (values * scale * norm_gain).astype(jnp.bfloat16)

def pack_branch(pack_rows, first_row, bundle_row_lengths, norm_gain, query_weight, keyval_weight, query_bias, keyval_bias, out_weight):
    row_count = pack_rows.shape[0]
    segment, position, starts, bundle_id = document_layout(bundle_row_lengths, first_row, row_count)
    normed = normalize(pack_rows, norm_gain)
    query_raw = jnp.dot(normed, query_weight, preferred_element_type=jnp.float32) + query_bias
    key_raw = jnp.dot(normed, keyval_weight[:, 0, :], preferred_element_type=jnp.float32) + keyval_bias[0]
    value_raw = jnp.dot(normed, keyval_weight[:, 1, :], preferred_element_type=jnp.float32) + keyval_bias[1]
    queries = rotate_heads(query_raw.reshape(row_count, HEADS, HD), position).astype(jnp.bfloat16)
    key_heads = rotate_heads(key_raw.reshape(row_count, KV, HD), position).astype(jnp.bfloat16)
    value_heads = value_raw.astype(jnp.bfloat16).reshape(row_count, KV, HD)
    grouped = queries.reshape(row_count, KV, HEADS // KV, HD)
    attention_scores = jnp.einsum('rkgd,skd->kgrs', grouped.astype(jnp.float32), key_heads.astype(jnp.float32)) * HD ** (-0.5)
    places = jnp.arange(row_count, dtype=jnp.int32)
    allowed = (segment[:, None] == segment[None, :]) & (places[None, :] <= places[:, None])
    attention_scores = jnp.where(allowed[None, None], attention_scores, -jnp.inf)
    highest = lax.optimization_barrier(jnp.max(attention_scores, axis=-1, keepdims=True))
    exponent = jnp.exp(attention_scores - highest)
    weights = (exponent / lax.optimization_barrier(jnp.sum(exponent, axis=-1, keepdims=True))).astype(jnp.bfloat16)
    context = jnp.einsum('kgrs,skd->rkgd', weights.astype(jnp.float32), value_heads.astype(jnp.float32))
    context = context.astype(jnp.bfloat16).reshape(row_count, HEADS * HD)
    group_cols = HEADS * HD // N_TENSOR
    summed = jnp.zeros((row_count, D), jnp.float32)
    for tensor_group in range(N_TENSOR):
        lower = tensor_group * group_cols
        partial_value = jnp.dot(context[:, lower:lower + group_cols], out_weight[lower:lower + group_cols], preferred_element_type=jnp.float32)
        summed = summed + partial_value.astype(jnp.bfloat16).astype(jnp.float32)
    return summed.astype(jnp.bfloat16)

def reference(hidden_in, norm_gain, query_weight, keyval_weight, query_bias, keyval_bias, out_weight, bundle_row_lengths, move_plan, first_len):
    packs = hidden_in.reshape(N_DP, TOK_GRP, D)

    def one_pack(inputs):
        pack_rows, first_row = inputs
        return pack_branch(pack_rows, first_row, bundle_row_lengths, norm_gain, query_weight, keyval_weight, query_bias, keyval_bias, out_weight)
    branches = lax.map(one_pack, (packs, first_len))
    bundle_id = document_layout(bundle_row_lengths, first_len[0], TOK_GRP)[3]
    places = jnp.arange(TOK_GRP, dtype=jnp.int32)
    shifts = jnp.take(move_plan, bundle_id).astype(jnp.int32)
    sources = ((jnp.arange(N_DP, dtype=jnp.int32)[:, None] - shifts[None, :]) % N_DP).astype(jnp.int32)
    return branches[sources, places[None, :]].reshape(N_DP * TOK_GRP, D)
```

```python
import jax
import jax.numpy as jnp
from jax import lax
from jax.sharding import Mesh, PartitionSpec as P

HD = 128
THETA = 1000000.0
EPS = 1e-06
BF = jnp.bfloat16
F32 = jnp.float32
DP = ("y", "z")


def ring(n, step):
    return [(i, (i + step) % n) for i in range(n)]


def hop(v, step):
    return lax.ppermute(v, "x", ring(lax.axis_size("x"), step))


def swap(v):
    return lax.ppermute(v, "c", [(0, 1), (1, 0)])


def dot(a, b):
    return jnp.dot(a, b, preferred_element_type=F32)


def rotate(values, cosines, sines):
    rows = values.shape[0]
    heads = values.reshape(rows, -1, HD)
    lower, upper = heads[..., : HD // 2], heads[..., HD // 2 :]
    cosines, sines = cosines[:, None, :], sines[:, None, :]
    turned = jnp.concatenate(
        [lower * cosines - upper * sines, upper * cosines + lower * sines], axis=-1
    )
    return turned.astype(BF)


def attend(queries, keys, values, allowed):
    scores = jnp.einsum("rgd,sd->grs", queries, keys, preferred_element_type=F32) * HD ** (-0.5)
    scores = jnp.where(allowed[None], scores, -jnp.inf)
    exponent = jnp.exp(scores - jnp.max(scores, axis=-1, keepdims=True))
    probs = (exponent / jnp.sum(exponent, axis=-1, keepdims=True)).astype(BF)
    context = jnp.einsum("grs,sd->rgd", probs, values, preferred_element_type=F32)
    return context.astype(BF)


def shards(
    hidden_in,
    norm_gain,
    query_weight,
    keyval_weight,
    query_bias,
    keyval_bias,
    out_weight,
    lengths,
    move_plan,
    first_len,
):
    packs = lax.axis_size(DP)
    pack = lax.axis_index(DP)
    x = lax.axis_index("x")
    core = lax.axis_index("c")
    nx = lax.axis_size("x")
    here = hidden_in.shape[0]
    width = hidden_in.shape[1]
    rows = here * nx * 2
    q_cols = query_weight.shape[1]

    combined = jnp.concatenate([query_weight, keyval_weight.reshape(keyval_weight.shape[0], -1)], axis=1)
    w_in = lax.all_gather(combined, DP, axis=0, tiled=True)

    values = hidden_in.astype(F32)
    scale = lax.rsqrt(jnp.mean(values * values, axis=1, keepdims=True) + EPS)
    own = (values * scale * norm_gain).astype(BF)
    half = width // 2
    left = hop(own, 1)
    right = hop(own, -1)
    far = jnp.concatenate([hop(left[:, :half], 1), hop(right[:, half:], -1)], axis=1)
    parts = []
    for part in (own, left, far, right):
        parts += [part, swap(part)]
    normed = jnp.concatenate(parts, axis=0)
    r = jnp.arange(here, dtype=jnp.int32)
    places = jnp.concatenate(
        [
            here * (2 * ((x - s) % nx) + (core if k == 0 else 1 - core)) + r
            for s in range(4)
            for k in range(2)
        ]
    )

    places_out = jnp.concatenate(
        [here * (2 * ((x - s) % nx) + k) + r for s in range(4) for k in range(2)]
    )

    ids = jnp.arange(lengths.shape[0], dtype=jnp.int32)
    offsets = jnp.cumsum(lengths) - lengths
    bundle = jnp.sum((places[:, None] >= offsets[None, :]).astype(jnp.int32), axis=1) - 1
    selector = (bundle[:, None] == ids[None, :]).astype(jnp.int32)
    starts = jnp.sum(selector * offsets[None, :], axis=1)
    first_here = jnp.sum(first_len * (jnp.arange(packs)[:, None] == pack).astype(jnp.int32), axis=0)
    splits = jnp.sum(selector * first_here[None, :], axis=1)
    second = (places - starts >= splits).astype(jnp.int32)
    segment = bundle * 2 + second
    position = (places - starts - second * splits).astype(F32)
    allowed = (segment[:, None] == segment[None, :]) & (places[None, :] <= places[:, None])
    indices = jnp.arange(HD // 2, dtype=F32)
    angles = position[:, None] * (THETA ** (-2.0 * indices / HD))[None, :]
    cosines, sines = jnp.cos(angles), jnp.sin(angles)

    cols = out_weight.shape[1] // 2
    w_low, w_high = out_weight[:, :cols], out_weight[:, cols:]
    mine = jnp.where(core == 0, w_low, w_high)
    other = swap(jnp.where(core == 0, w_high, w_low))
    w_both = jnp.concatenate([mine, other], axis=0)
    w_both, left_tie = lax.optimization_barrier((w_both, left))
    chunks = 2
    step = cols // chunks
    w_out = [
        lax.all_gather(w_both[:, j * step : (j + 1) * step], DP, axis=0, tiled=False)
        for j in range(chunks)
    ]

    projected = dot(normed, w_in)
    queries = rotate(projected[:, :q_cols] + query_bias, cosines, sines)
    keys = rotate(projected[:, q_cols : q_cols + HD] + keyval_bias[0], cosines, sines)[:, 0]
    vals = (projected[:, q_cols + HD :] + keyval_bias[1]).astype(BF)
    context = attend(queries, keys, vals, allowed).reshape(rows, q_cols)

    capacity = 2 * rows // packs
    lanes = jnp.arange(capacity, dtype=jnp.int32)
    slots = jnp.arange(packs, dtype=jnp.int32)
    outgoing = (move_plan[None, :] == ((slots - pack) % packs)[:, None]).astype(jnp.int32)
    send_start = jnp.sum(outgoing * offsets[None, :], axis=1)
    send_length = jnp.sum(outgoing * lengths[None, :], axis=1)
    live = lanes[None, :] < send_length[:, None]
    send_rows = jnp.where(live, send_start[:, None] + lanes[None, :], -1).reshape(-1)
    pick = (send_rows[:, None] == places[None, :]).astype(BF)
    sent = dot(pick, context).astype(BF).reshape(packs, capacity, q_cols)
    got = lax.all_to_all(sent, DP, split_axis=0, concat_axis=0, tiled=True)
    sources = (pack - move_plan) % packs
    bundle_out = jnp.sum((places_out[:, None] >= offsets[None, :]).astype(jnp.int32), axis=1) - 1
    selector = (bundle_out[:, None] == ids[None, :]).astype(jnp.int32)
    source = jnp.sum(selector * sources[None, :], axis=1)
    slot = source * capacity + places_out - jnp.sum(selector * offsets[None, :], axis=1)
    place = (slot[:, None] == jnp.arange(packs * capacity, dtype=jnp.int32)[None, :]).astype(BF)
    moved = dot(place, got.reshape(packs * capacity, q_cols)).astype(BF)
    both = jnp.concatenate([moved, swap(moved)], axis=1)

    outs = []
    block = 2 * here
    for j in range(chunks):
        partial = jnp.concatenate([dot(both, w_out[j][d]).astype(BF) for d in range(packs)], axis=1)
        part = [partial[s * block : (s + 1) * block] for s in range(4)]
        mid = part[0].shape[1] // 2
        a = hop(part[2][:, :mid], 1)
        b = hop(part[2][:, mid:], -1)
        up = jnp.concatenate(
            [(part[3][:, :mid].astype(F32) + a.astype(F32)).astype(BF), part[3][:, mid:]], axis=1
        )
        down = jnp.concatenate(
            [part[1][:, :mid], (part[1][:, mid:].astype(F32) + b.astype(F32)).astype(BF)], axis=1
        )
        u, v = hop(up, 1), hop(down, -1)
        total = (part[0].astype(F32) + u.astype(F32) + v.astype(F32)).astype(BF)
        mine = jnp.where(core == 0, total[:here], total[here:])
        other = swap(jnp.where(core == 0, total[here:], total[:here]))
        mine, other = mine.reshape(here, packs, 1, step), other.reshape(here, packs, 1, step)
        outs.append(
            jnp.concatenate(
                [jnp.where(core == 0, mine, other), jnp.where(core == 0, other, mine)], axis=2
            )
        )
    out = jnp.stack(outs, axis=3)
    return out.reshape(here, width)


def solution(mesh):
    packs, tensor = mesh.devices.shape
    side = int(round(packs**0.5))
    fine = Mesh(mesh.devices.reshape(side, packs // side, tensor // 2, 2), ("y", "z", "x", "c"))
    every = ("y", "z", "x", "c")
    heads = ("x", "c")
    in_specs = (
        P(every, None),
        P(),
        P(DP, heads),
        P(DP, None, heads),
        P(heads),
        P(None, heads),
        P(heads, DP),
        P(),
        P(),
        P(),
    )
    return jax.shard_map(
        shards, mesh=fine, in_specs=in_specs, out_specs=P(every, None), check_vma=False
    )
```

```python
import jax
import jax.numpy as jnp
from jax import lax
from jax.sharding import Mesh, PartitionSpec as P

HD = 128
THETA = 1000000.0
EPS = 1e-06
BF = jnp.bfloat16
F32 = jnp.float32
DP = ("y", "z")


def ring(n, step):
    return [(i, (i + step) % n) for i in range(n)]


def hop(v, axis, step):
    return lax.ppermute(v, axis, ring(lax.axis_size(axis), step))


def swap(v):
    return lax.ppermute(v, "c", [(0, 1), (1, 0)])


def dot(a, b):
    return jnp.dot(a, b, preferred_element_type=F32)


def rotate(values, cosines, sines):
    rows = values.shape[0]
    heads = values.reshape(rows, -1, HD)
    lower, upper = heads[..., : HD // 2], heads[..., HD // 2 :]
    cosines, sines = cosines[:, None, :], sines[:, None, :]
    turned = jnp.concatenate(
        [lower * cosines - upper * sines, upper * cosines + lower * sines], axis=-1
    )
    return turned.astype(BF)


def attend(queries, keys, values, allowed):
    scores = jnp.einsum("rgd,sd->grs", queries, keys, preferred_element_type=F32) * HD ** (-0.5)
    scores = jnp.where(allowed[None], scores, -jnp.inf)
    exponent = jnp.exp(scores - jnp.max(scores, axis=-1, keepdims=True))
    probs = (exponent / jnp.sum(exponent, axis=-1, keepdims=True)).astype(BF)
    context = jnp.einsum("grs,sd->rgd", probs, values, preferred_element_type=F32)
    return context.astype(BF)


def shards(
    hidden_in,
    norm_gain,
    query_weight,
    keyval_weight,
    query_bias,
    keyval_bias,
    out_weight,
    lengths,
    move_plan,
    first_len,
):
    packs = lax.axis_size(DP)
    pack = lax.axis_index(DP)
    x = lax.axis_index("x")
    y = lax.axis_index("y")
    core = lax.axis_index("c")
    nx = lax.axis_size("x")
    ny = lax.axis_size("y")
    here = hidden_in.shape[0]
    width = hidden_in.shape[1]
    rows = here * nx * 2
    q_cols = query_weight.shape[1]

    combined = jnp.concatenate([query_weight, keyval_weight.reshape(keyval_weight.shape[0], -1)], axis=1)
    w_in = lax.all_gather(combined, "z", axis=0, tiled=True)
    block = width // ny
    half = block // 2

    values = hidden_in.astype(F32)
    scale = lax.rsqrt(jnp.mean(values * values, axis=1, keepdims=True) + EPS)
    own = (values * scale * norm_gain).astype(BF)

    def features(step):
        return lax.dynamic_slice_in_dim(own, (y + step) % ny * block, block, axis=1)

    pack_0 = features(0)
    pack_2 = hop(features(2), "y", 2)
    pack_m = hop(features(1), "y", 1)
    pack_p = hop(features(-1), "y", -1)

    def project(chunks):
        count = len(chunks)
        v = jnp.concatenate(chunks, axis=0)
        left = hop(v, "x", 1)
        right = hop(v, "x", -1)
        far = jnp.concatenate(
            [hop(left[:, :half], "x", 1), hop(right[:, half:], "x", -1)], axis=1
        )
        m = jnp.concatenate(
            [t[i * here : (i + 1) * here] for i in range(count) for t in (v, left, far, right)], axis=0
        )
        o = swap(m)
        size = here * nx
        return [
            jnp.concatenate(
                [dot(t[i * size : (i + 1) * size], w_in) for t in (m, o)], axis=0
            )
            for i in range(count)
        ]

    (sum_0,) = project([pack_0])
    (sum_2,) = project([pack_2])
    sum_m, sum_p = project([pack_m, pack_p])

    mid = sum_0.shape[1] // 2
    two = sum_2.astype(BF)
    a = hop(two[:, :mid], "y", 1)
    b = hop(two[:, mid:], "y", -1)
    up = jnp.concatenate(
        [(sum_p[:, :mid] + a.astype(F32)).astype(BF), sum_p[:, mid:].astype(BF)], axis=1
    )
    down = jnp.concatenate(
        [sum_m[:, :mid].astype(BF), (sum_m[:, mid:] + b.astype(F32)).astype(BF)], axis=1
    )
    from_m = hop(up, "y", 1)
    from_p = hop(down, "y", -1)
    projected = sum_0 + from_m.astype(F32) + from_p.astype(F32)

    r = jnp.arange(here, dtype=jnp.int32)
    places = jnp.concatenate(
        [
            here * (2 * ((x - s) % nx) + (core if k == 0 else 1 - core)) + r
            for k in range(2)
            for s in range(4)
        ]
    )
    places_out = jnp.concatenate(
        [here * (2 * ((x - s) % nx) + k) + r for s in range(4) for k in range(2)]
    )

    ids = jnp.arange(lengths.shape[0], dtype=jnp.int32)
    offsets = jnp.cumsum(lengths) - lengths
    bundle = jnp.sum((places[:, None] >= offsets[None, :]).astype(jnp.int32), axis=1) - 1
    selector = (bundle[:, None] == ids[None, :]).astype(jnp.int32)
    starts = jnp.sum(selector * offsets[None, :], axis=1)
    first_here = jnp.sum(first_len * (jnp.arange(packs)[:, None] == pack).astype(jnp.int32), axis=0)
    splits = jnp.sum(selector * first_here[None, :], axis=1)
    second = (places - starts >= splits).astype(jnp.int32)
    segment = bundle * 2 + second
    position = (places - starts - second * splits).astype(F32)
    allowed = (segment[:, None] == segment[None, :]) & (places[None, :] <= places[:, None])
    indices = jnp.arange(HD // 2, dtype=F32)
    angles = position[:, None] * (THETA ** (-2.0 * indices / HD))[None, :]
    cosines, sines = jnp.cos(angles), jnp.sin(angles)

    cols = out_weight.shape[1] // 2
    w_low, w_high = out_weight[:, :cols], out_weight[:, cols:]
    mine = jnp.where(core == 0, w_low, w_high)
    other = swap(jnp.where(core == 0, w_high, w_low))
    w_both = jnp.concatenate([mine, other], axis=0)
    w_out = lax.all_gather(w_both, DP, axis=0, tiled=False)

    queries = rotate(projected[:, :q_cols] + query_bias, cosines, sines)
    keys = rotate(projected[:, q_cols : q_cols + HD] + keyval_bias[0], cosines, sines)[:, 0]
    vals = (projected[:, q_cols + HD :] + keyval_bias[1]).astype(BF)
    context = attend(queries, keys, vals, allowed).reshape(rows, q_cols)

    capacity = 2 * rows // packs
    lanes = jnp.arange(capacity, dtype=jnp.int32)
    slots = jnp.arange(packs, dtype=jnp.int32)
    outgoing = (move_plan[None, :] == ((slots - pack) % packs)[:, None]).astype(jnp.int32)
    send_start = jnp.sum(outgoing * offsets[None, :], axis=1)
    send_length = jnp.sum(outgoing * lengths[None, :], axis=1)
    live = lanes[None, :] < send_length[:, None]
    send_rows = jnp.where(live, send_start[:, None] + lanes[None, :], -1).reshape(-1)
    pick = (send_rows[:, None] == places[None, :]).astype(BF)
    sent = dot(pick, context).astype(BF).reshape(packs, capacity, q_cols)
    got = lax.all_to_all(sent, DP, split_axis=0, concat_axis=0, tiled=True)
    sources = (pack - move_plan) % packs
    bundle_out = jnp.sum((places_out[:, None] >= offsets[None, :]).astype(jnp.int32), axis=1) - 1
    selector = (bundle_out[:, None] == ids[None, :]).astype(jnp.int32)
    source = jnp.sum(selector * sources[None, :], axis=1)
    slot = source * capacity + places_out - jnp.sum(selector * offsets[None, :], axis=1)
    place = (slot[:, None] == jnp.arange(packs * capacity, dtype=jnp.int32)[None, :]).astype(BF)
    moved = dot(place, got.reshape(packs * capacity, q_cols)).astype(BF)
    both = jnp.concatenate([moved, swap(moved)], axis=1)

    totals = []
    pair = 2 * here
    chunks = 2
    for j in range(chunks):
        count = packs // chunks
        partial = jnp.concatenate(
            [dot(both, w_out[j * count + d]).astype(BF) for d in range(count)], axis=1
        )
        part = [partial[s * pair : (s + 1) * pair] for s in range(4)]
        mid = part[0].shape[1] // 2
        a = hop(part[2][:, :mid], "x", 1)
        b = hop(part[2][:, mid:], "x", -1)
        up = jnp.concatenate(
            [(part[3][:, :mid].astype(F32) + a.astype(F32)).astype(BF), part[3][:, mid:]], axis=1
        )
        down = jnp.concatenate(
            [part[1][:, :mid], (part[1][:, mid:].astype(F32) + b.astype(F32)).astype(BF)], axis=1
        )
        u, v = hop(up, "x", 1), hop(down, "x", -1)
        totals.append((part[0].astype(F32) + u.astype(F32) + v.astype(F32)).astype(BF))
    total = jnp.concatenate(totals, axis=1)
    mine = jnp.where(core == 0, total[:here], total[here:])
    other = swap(jnp.where(core == 0, total[here:], total[:here]))
    mine, other = mine.reshape(here, packs, 1, cols), other.reshape(here, packs, 1, cols)
    out = jnp.concatenate(
        [jnp.where(core == 0, mine, other), jnp.where(core == 0, other, mine)], axis=2
    )
    return out.reshape(here, width)


def solution(mesh):
    packs, tensor = mesh.devices.shape
    side = int(round(packs**0.5))
    fine = Mesh(mesh.devices.reshape(side, packs // side, tensor // 2, 2), ("y", "z", "x", "c"))
    every = ("y", "z", "x", "c")
    heads = ("x", "c")
    in_specs = (
        P(every, None),
        P(),
        P(DP, heads),
        P(DP, None, heads),
        P(heads),
        P(None, heads),
        P(heads, DP),
        P(),
        P(),
        P(),
    )
    return jax.shard_map(
        shards, mesh=fine, in_specs=in_specs, out_specs=P(every, None), check_vma=False
    )
```

```python
import functools

import jax
import jax.numpy as jnp
from jax import lax
from jax.experimental import pallas as pl
from jax.experimental.pallas import tpu as pltpu
from jax.sharding import Mesh, PartitionSpec as P

HD = 128
THETA = 1000000.0
EPS = 1e-06
BF = jnp.bfloat16
F32 = jnp.float32
DP = ("y", "z")


def ring(n, step):
    return [(i, (i + step) % n) for i in range(n)]


def hop(v, axis, step):
    with jax.named_scope(f"{axis}{step % lax.axis_size(axis)}"):
        return lax.ppermute(v, axis, ring(lax.axis_size(axis), step))


def swap(v):
    with jax.named_scope("core"):
        return lax.ppermute(v, "c", [(0, 1), (1, 0)])


def dot(a, b):
    return jnp.dot(a, b, preferred_element_type=F32)


def attend_kernel(here, heads, core_ref, sum_ref, m_ref, p_ref, bias_ref, cos_ref, sin_ref, back_ref,
                  place_ref, send_ref, out_ref, proj, keys, vals, context):
    rows = sum_ref.shape[0]
    q_cols = heads * HD
    proj[...] = sum_ref[...] + m_ref[...].astype(F32) + p_ref[...].astype(F32) + bias_ref[...]

    def turned(u, at):
        swapped = jnp.concatenate([u[:, HD // 2 :], u[:, : HD // 2]], axis=1)
        return u * cos_ref[at, :] + swapped * sin_ref[at, :]

    every = pl.ds(0, rows)
    keys[...] = turned(proj[:, q_cols : q_cols + HD], every).astype(BF).astype(F32)
    vals[...] = proj[:, q_cols + HD :].astype(BF).astype(F32)
    core = core_ref[0]
    chips = rows // (2 * here)
    lane = lax.broadcasted_iota(jnp.int32, (here, 2 * here), 1)
    own = here + lax.broadcasted_iota(jnp.int32, (here, 2 * here), 0)
    for k in range(2):
        c = core if k == 0 else 1 - core
        for s in range(chips):
            at = pl.ds((k * chips + s) * here, here)
            before = pl.ds(pl.multiple_of(((1 - k) * chips + lax.rem(s + 1 - c, chips)) * here, 8), here)
            ks = jnp.concatenate([keys[before, :], keys[at, :]], axis=0).astype(BF)
            vs = jnp.concatenate([vals[before, :], vals[at, :]], axis=0).astype(BF)
            q = jnp.concatenate(
                [turned(proj[at, h * HD : (h + 1) * HD], at) for h in range(heads)], axis=0
            ).astype(BF)
            scores = lax.dot_general(q, ks, (((1,), (1,)), ((), ())), preferred_element_type=F32)
            allowed = (lane <= own) & (lane >= own - back_ref[at, :])
            allowed = jnp.concatenate([allowed.astype(jnp.int32)] * heads, axis=0) > 0
            scores = jnp.where(allowed, scores * HD ** (-0.5), -jnp.inf)
            e = jnp.exp(scores - jnp.max(scores, axis=1, keepdims=True))
            probs = (e / jnp.sum(e, axis=1, keepdims=True)).astype(BF)
            ctx = jnp.dot(probs, vs, preferred_element_type=F32)
            for h in range(heads):
                context[at, h * HD : (h + 1) * HD] = ctx[h * here : (h + 1) * here]
    ctx = context[...].astype(BF)
    step = out_ref.shape[0] // 4
    for i in range(4):
        at = pl.ds(i * step, step)
        pick = jnp.where(send_ref[at, :] == place_ref[...], 1.0, 0.0).astype(BF)
        out_ref[at, :] = jnp.dot(pick, ctx, preferred_element_type=F32).astype(BF)


def attend(here, heads, slots, core, total, part_m, part_p, bias, cosines, sines, back, places, send_rows):
    rows, cols = total.shape
    vmem = pl.BlockSpec(memory_space=pltpu.VMEM)
    return pl.pallas_call(
        functools.partial(attend_kernel, here, heads),
        out_shape=jax.ShapeDtypeStruct((slots, heads * HD), BF),
        in_specs=[pl.BlockSpec(memory_space=pltpu.SMEM)] + [vmem] * 9,
        out_specs=vmem,
        scratch_shapes=[
            pltpu.VMEM((rows, cols), F32),
            pltpu.VMEM((rows, HD), F32),
            pltpu.VMEM((rows, HD), F32),
            pltpu.VMEM((rows, heads * HD), F32),
        ],
        compiler_params=pltpu.CompilerParams(vmem_limit_bytes=40 * 1024 * 1024),
        cost_estimate=pl.CostEstimate(flops=1 << 30, bytes_accessed=8 << 20, transcendentals=1 << 20),
    )(core, total, part_m, part_p, bias, cosines, sines, back, places, send_rows)


def shards(
    hidden_in,
    norm_gain,
    query_weight,
    keyval_weight,
    query_bias,
    keyval_bias,
    out_weight,
    lengths,
    move_plan,
    first_len,
):
    packs = lax.axis_size(DP)
    pack = lax.axis_index(DP)
    x = lax.axis_index("x")
    y = lax.axis_index("y")
    core = lax.axis_index("c")
    nx = lax.axis_size("x")
    ny = lax.axis_size("y")
    z = lax.axis_index("z")
    nz = lax.axis_size("z")
    here = hidden_in.shape[0]
    width = hidden_in.shape[1]
    rows = here * nx * 2
    q_cols = query_weight.shape[1]

    combined = jnp.concatenate([query_weight, keyval_weight.reshape(keyval_weight.shape[0], -1)], axis=1)
    deep = combined.shape[0] // 2
    with jax.named_scope("w_in"):
        w_prev, w_next = hop(combined, "z", 1), hop(combined, "z", -1)
        w_far = [hop(w_next[:deep], "z", -1), hop(w_prev[deep:], "z", 1)]
    w_in = jnp.concatenate([combined, w_next, *w_far, w_prev], axis=0)
    block = width // ny
    half = block // 2

    values = hidden_in.astype(F32)
    scale = lax.rsqrt(jnp.mean(values * values, axis=1, keepdims=True) + EPS)
    own = (values * scale * norm_gain).astype(BF)

    def features(step):
        share = block // nz
        first = (y + step) % ny * block
        return jnp.concatenate(
            [
                lax.dynamic_slice_in_dim(own, first + (z + i) % nz * share, share, axis=1)
                for i in range(nz)
            ],
            axis=1,
        )

    with jax.named_scope("exchange"):
        pack_0 = features(0)
        pack_2 = hop(features(2), "y", 2)
        pack_m = hop(features(1), "y", 1)
        pack_p = hop(features(-1), "y", -1)

    def project(chunks):
        count = len(chunks)
        v = jnp.concatenate(chunks, axis=0)
        left = hop(v, "x", 1)
        right = hop(v, "x", -1)
        far = jnp.concatenate(
            [hop(left[:, :half], "x", 1), hop(right[:, half:], "x", -1)], axis=1
        )
        m = jnp.concatenate(
            [t[i * here : (i + 1) * here] for i in range(count) for t in (v, left, far, right)], axis=0
        )
        o = swap(m)
        size = here * nx
        return [
            jnp.concatenate(
                [dot(t[i * size : (i + 1) * size], w_in) for t in (m, o)], axis=0
            )
            for i in range(count)
        ]

    with jax.named_scope("own"):
        (sum_0,) = project([pack_0])
    with jax.named_scope("opposite"):
        (sum_2,) = project([pack_2])
    with jax.named_scope("sides"):
        sum_m, sum_p = project([pack_m, pack_p])

    mid = sum_0.shape[1] // 2
    two = sum_2.astype(BF)
    a = hop(two[:, :mid], "y", 1)
    b = hop(two[:, mid:], "y", -1)
    up = jnp.concatenate(
        [(sum_p[:, :mid] + a.astype(F32)).astype(BF), sum_p[:, mid:].astype(BF)], axis=1
    )
    down = jnp.concatenate(
        [sum_m[:, :mid].astype(BF), (sum_m[:, mid:] + b.astype(F32)).astype(BF)], axis=1
    )
    from_m = hop(up, "y", 1)
    from_p = hop(down, "y", -1)

    r = jnp.arange(here, dtype=jnp.int32)
    places = jnp.concatenate(
        [
            here * (2 * ((x - s) % nx) + (core if k == 0 else 1 - core)) + r
            for k in range(2)
            for s in range(4)
        ]
    )
    places_out = jnp.concatenate(
        [here * (2 * ((x - s) % nx) + k) + r for s in range(4) for k in range(2)]
    )

    ids = jnp.arange(lengths.shape[0], dtype=jnp.int32)
    offsets = jnp.cumsum(lengths) - lengths
    bundle = jnp.sum((places[:, None] >= offsets[None, :]).astype(jnp.int32), axis=1) - 1
    selector = (bundle[:, None] == ids[None, :]).astype(jnp.int32)
    starts = jnp.sum(selector * offsets[None, :], axis=1)
    first_here = jnp.sum(first_len * (jnp.arange(packs)[:, None] == pack).astype(jnp.int32), axis=0)
    splits = jnp.sum(selector * first_here[None, :], axis=1)
    back = places - starts
    back = back - jnp.where(back >= splits, splits, 0)
    indices = jnp.arange(HD // 2, dtype=F32)
    angles = back.astype(F32)[:, None] * (THETA ** (-2.0 * indices / HD))[None, :]
    cosines, sines = jnp.cos(angles), jnp.sin(angles)
    cosines = jnp.concatenate([cosines, cosines], axis=1)
    sines = jnp.concatenate([-sines, sines], axis=1)

    cols = out_weight.shape[1] // 2
    w_low, w_high = out_weight[:, :cols], out_weight[:, cols:]
    mine = jnp.where(core == 0, w_low, w_high)
    other = swap(jnp.where(core == 0, w_high, w_low))
    w_both = jnp.concatenate([mine, other], axis=0)
    w_out = lax.all_gather(w_both, DP, axis=0, tiled=False)

    capacity = 2 * rows // packs
    lanes = jnp.arange(capacity, dtype=jnp.int32)
    slots = jnp.arange(packs, dtype=jnp.int32)
    outgoing = (move_plan[None, :] == ((slots - pack) % packs)[:, None]).astype(jnp.int32)
    send_start = jnp.sum(outgoing * offsets[None, :], axis=1)
    send_length = jnp.sum(outgoing * lengths[None, :], axis=1)
    live = lanes[None, :] < send_length[:, None]
    send_rows = jnp.where(live, send_start[:, None] + lanes[None, :], -1).reshape(-1)
    bias = jnp.concatenate([query_bias, keyval_bias.reshape(-1)])[None, :]
    sent = attend(
        here,
        q_cols // HD,
        packs * capacity,
        core.reshape(1),
        sum_0,
        from_m,
        from_p,
        bias,
        cosines,
        sines,
        back[:, None],
        places[None, :],
        send_rows[:, None],
    ).reshape(packs, capacity, q_cols)
    got = lax.all_to_all(sent, DP, split_axis=0, concat_axis=0, tiled=True)
    sources = (pack - move_plan) % packs
    bundle_out = jnp.sum((places_out[:, None] >= offsets[None, :]).astype(jnp.int32), axis=1) - 1
    selector = (bundle_out[:, None] == ids[None, :]).astype(jnp.int32)
    source = jnp.sum(selector * sources[None, :], axis=1)
    slot = source * capacity + places_out - jnp.sum(selector * offsets[None, :], axis=1)
    place = (slot[:, None] == jnp.arange(packs * capacity, dtype=jnp.int32)[None, :]).astype(BF)
    moved = dot(place, got.reshape(packs * capacity, q_cols)).astype(BF)
    both = jnp.concatenate([moved, swap(moved)], axis=1)

    totals = []
    pair = 2 * here
    chunks = 2
    for j in range(chunks):
        count = packs // chunks
        partial = jnp.concatenate(
            [dot(both, w_out[j * count + d]).astype(BF) for d in range(count)], axis=1
        )
        part = [partial[s * pair : (s + 1) * pair] for s in range(4)]
        mid = part[0].shape[1] // 2
        a = hop(part[2][:, :mid], "x", 1)
        b = hop(part[2][:, mid:], "x", -1)
        up = jnp.concatenate(
            [(part[3][:, :mid].astype(F32) + a.astype(F32)).astype(BF), part[3][:, mid:]], axis=1
        )
        down = jnp.concatenate(
            [part[1][:, :mid], (part[1][:, mid:].astype(F32) + b.astype(F32)).astype(BF)], axis=1
        )
        u, v = hop(up, "x", 1), hop(down, "x", -1)
        totals.append((part[0].astype(F32) + u.astype(F32) + v.astype(F32)).astype(BF))
    total = jnp.concatenate(totals, axis=1)
    mine = jnp.where(core == 0, total[:here], total[here:])
    other = swap(jnp.where(core == 0, total[here:], total[:here]))
    mine, other = mine.reshape(here, packs, 1, cols), other.reshape(here, packs, 1, cols)
    out = jnp.concatenate(
        [jnp.where(core == 0, mine, other), jnp.where(core == 0, other, mine)], axis=2
    )
    return out.reshape(here, width)


def solution(mesh):
    packs, tensor = mesh.devices.shape
    side = int(round(packs**0.5))
    fine = Mesh(mesh.devices.reshape(side, packs // side, tensor // 2, 2), ("y", "z", "x", "c"))
    every = ("y", "z", "x", "c")
    heads = ("x", "c")
    in_specs = (
        P(every, None),
        P(),
        P(DP, heads),
        P(DP, None, heads),
        P(heads),
        P(None, heads),
        P(heads, DP),
        P(),
        P(),
        P(),
    )
    return jax.shard_map(
        shards, mesh=fine, in_specs=in_specs, out_specs=P(every, None), check_vma=False
    )
```

```python
import functools

import jax
import jax.numpy as jnp
from jax import lax
from jax.experimental import pallas as pl
from jax.experimental.pallas import tpu as pltpu
from jax.sharding import Mesh, PartitionSpec as P

HD = 128
THETA = 1000000.0
EPS = 1e-06
BF = jnp.bfloat16
F32 = jnp.float32
DP = ("y", "z")


def ring(n, step):
    return [(i, (i + step) % n) for i in range(n)]


def hop(v, axis, step):
    with jax.named_scope(f"{axis}{step % lax.axis_size(axis)}"):
        return lax.ppermute(v, axis, ring(lax.axis_size(axis), step))


def swap(v):
    with jax.named_scope("core"):
        return lax.ppermute(v, "c", [(0, 1), (1, 0)])


def after(*values):
    return lax.optimization_barrier(values)


def dot(a, b):
    return jnp.dot(a, b, preferred_element_type=F32)


def attend_kernel(here, heads, core_ref, sum_ref, m_ref, p_ref, bias_ref, cos_ref, sin_ref, back_ref,
                  place_ref, send_ref, out_ref, proj, keys, vals, context):
    rows = sum_ref.shape[0]
    q_cols = heads * HD
    proj[...] = sum_ref[...] + m_ref[...].astype(F32) + p_ref[...].astype(F32) + bias_ref[...]

    def turned(u, at):
        swapped = jnp.concatenate([u[:, HD // 2 :], u[:, : HD // 2]], axis=1)
        return u * cos_ref[at, :] + swapped * sin_ref[at, :]

    every = pl.ds(0, rows)
    keys[...] = turned(proj[:, q_cols : q_cols + HD], every).astype(BF).astype(F32)
    vals[...] = proj[:, q_cols + HD :].astype(BF).astype(F32)
    core = core_ref[0]
    chips = rows // (2 * here)
    lane = lax.broadcasted_iota(jnp.int32, (here, 2 * here), 1)
    own = here + lax.broadcasted_iota(jnp.int32, (here, 2 * here), 0)
    for k in range(2):
        c = core if k == 0 else 1 - core
        for s in range(chips):
            at = pl.ds((k * chips + s) * here, here)
            before = pl.ds(pl.multiple_of(((1 - k) * chips + lax.rem(s + 1 - c, chips)) * here, 8), here)
            ks = jnp.concatenate([keys[before, :], keys[at, :]], axis=0).astype(BF)
            vs = jnp.concatenate([vals[before, :], vals[at, :]], axis=0).astype(BF)
            q = jnp.concatenate(
                [turned(proj[at, h * HD : (h + 1) * HD], at) for h in range(heads)], axis=0
            ).astype(BF)
            scores = lax.dot_general(q, ks, (((1,), (1,)), ((), ())), preferred_element_type=F32)
            allowed = (lane <= own) & (lane >= own - back_ref[at, :])
            allowed = jnp.concatenate([allowed.astype(jnp.int32)] * heads, axis=0) > 0
            scores = jnp.where(allowed, scores * HD ** (-0.5), -jnp.inf)
            e = jnp.exp(scores - jnp.max(scores, axis=1, keepdims=True))
            probs = (e / jnp.sum(e, axis=1, keepdims=True)).astype(BF)
            ctx = jnp.dot(probs, vs, preferred_element_type=F32)
            for h in range(heads):
                context[at, h * HD : (h + 1) * HD] = ctx[h * here : (h + 1) * here]
    ctx = context[...].astype(BF)
    step = out_ref.shape[0] // 4
    for i in range(4):
        at = pl.ds(i * step, step)
        pick = jnp.where(send_ref[at, :] == place_ref[...], 1.0, 0.0).astype(BF)
        out_ref[at, :] = jnp.dot(pick, ctx, preferred_element_type=F32).astype(BF)


def attend(here, heads, slots, core, total, part_m, part_p, bias, cosines, sines, back, places, send_rows):
    rows, cols = total.shape
    vmem = pl.BlockSpec(memory_space=pltpu.VMEM)
    return pl.pallas_call(
        functools.partial(attend_kernel, here, heads),
        out_shape=jax.ShapeDtypeStruct((slots, heads * HD), BF),
        in_specs=[pl.BlockSpec(memory_space=pltpu.SMEM)] + [vmem] * 9,
        out_specs=vmem,
        scratch_shapes=[
            pltpu.VMEM((rows, cols), F32),
            pltpu.VMEM((rows, HD), F32),
            pltpu.VMEM((rows, HD), F32),
            pltpu.VMEM((rows, heads * HD), F32),
        ],
        compiler_params=pltpu.CompilerParams(vmem_limit_bytes=40 * 1024 * 1024),
        cost_estimate=pl.CostEstimate(flops=1 << 30, bytes_accessed=8 << 20, transcendentals=1 << 20),
    )(core, total, part_m, part_p, bias, cosines, sines, back, places, send_rows)


def multiply_kernel(sizes, w_ref, *refs):
    at = 0
    outs = refs[sum(sizes) :]
    for count, out_ref in zip(sizes, outs):
        total, depth = 0.0, 0
        for ref in refs[at : at + count]:
            total += jnp.dot(
                ref[...], w_ref[depth : depth + ref.shape[1]], preferred_element_type=F32
            )
            depth += ref.shape[1]
        out_ref[...] = total
        at += count


def multiply(products, w):
    flat = [t for pieces in products for t in pieces]
    vmem = pl.BlockSpec(memory_space=pltpu.VMEM)
    return pl.pallas_call(
        functools.partial(multiply_kernel, [len(pieces) for pieces in products]),
        out_shape=[jax.ShapeDtypeStruct((p[0].shape[0], w.shape[1]), F32) for p in products],
        in_specs=[vmem] * (1 + len(flat)),
        out_specs=[vmem] * len(products),
        compiler_params=pltpu.CompilerParams(vmem_limit_bytes=32 * 1024 * 1024),
        cost_estimate=pl.CostEstimate(flops=1 << 20, bytes_accessed=1 << 12, transcendentals=0),
    )(w, *flat)


def project_out_kernel(mine_ref, theirs_ref, w_ref, out_ref):
    both = jnp.concatenate([mine_ref[...], theirs_ref[...]], axis=1)
    w = jnp.concatenate([w_ref[i] for i in range(w_ref.shape[0])], axis=1)
    out_ref[...] = jnp.dot(both, w, preferred_element_type=F32).astype(BF)


def project_out(first, count, mine, theirs, w):
    rows, depth = mine.shape
    _, deep, width = w.shape
    group = 2
    whole = pl.BlockSpec((rows, depth), lambda d: (0, 0))
    return pl.pallas_call(
        project_out_kernel,
        out_shape=jax.ShapeDtypeStruct((rows, count * width), BF),
        grid=(count // group,),
        in_specs=[whole, whole, pl.BlockSpec((group, deep, width), lambda d: (first // group + d, 0, 0))],
        out_specs=pl.BlockSpec((rows, group * width), lambda d: (0, d)),
        compiler_params=pltpu.CompilerParams(vmem_limit_bytes=48 * 1024 * 1024),
        cost_estimate=pl.CostEstimate(
            flops=2 * rows * deep * width * count, bytes_accessed=8 << 20, transcendentals=0
        ),
    )(mine, theirs, w)


def interleave_kernel(side, width, at_ref, *refs):
    *parts, out_ref = refs
    core, y = at_ref[0], at_ref[1]
    blocks = parts[0].shape[1] // width
    for j in range(len(parts) // 2):
        for i in range(blocks):
            z, back = divmod(j * blocks + i, side)
            at = lax.rem(y + side - back, side) * side + z
            for part, c in ((parts[2 * j], core), (parts[2 * j + 1], 1 - core)):
                to = pl.multiple_of((at * 2 + c) * width, width)
                out_ref[:, pl.ds(to, width)] = part[:, i * width : (i + 1) * width]


def interleave(side, width, at, parts):
    rows, cols = parts[0].shape
    vmem = pl.BlockSpec(memory_space=pltpu.VMEM)
    return pl.pallas_call(
        functools.partial(interleave_kernel, side, width),
        out_shape=jax.ShapeDtypeStruct((rows, cols * len(parts)), BF),
        in_specs=[pl.BlockSpec(memory_space=pltpu.SMEM)] + [vmem] * len(parts),
        out_specs=vmem,
    )(at, *parts)


def shards(
    hidden_in,
    norm_gain,
    query_weight,
    keyval_weight,
    query_bias,
    keyval_bias,
    out_weight,
    lengths,
    move_plan,
    first_len,
):
    packs = lax.axis_size(DP)
    pack = lax.axis_index(DP)
    x = lax.axis_index("x")
    y = lax.axis_index("y")
    core = lax.axis_index("c")
    nx = lax.axis_size("x")
    ny = lax.axis_size("y")
    z = lax.axis_index("z")
    nz = lax.axis_size("z")
    here = hidden_in.shape[0]
    width = hidden_in.shape[1]
    rows = here * nx * 2
    q_cols = query_weight.shape[1]

    r = jnp.arange(here, dtype=jnp.int32)
    places = jnp.concatenate(
        [
            here * (2 * ((x - s) % nx) + (core if k == 0 else 1 - core)) + r
            for k in range(2)
            for s in range(4)
        ]
    )
    places_out = jnp.concatenate(
        [here * (2 * ((x - s) % nx) + k) + r for s in range(4) for k in range(2)]
    )

    ids = jnp.arange(lengths.shape[0], dtype=jnp.int32)
    offsets = jnp.cumsum(lengths) - lengths
    bundle = jnp.sum((places[:, None] >= offsets[None, :]).astype(jnp.int32), axis=1) - 1
    selector = (bundle[:, None] == ids[None, :]).astype(jnp.int32)
    starts = jnp.sum(selector * offsets[None, :], axis=1)
    first_here = jnp.sum(first_len * (jnp.arange(packs)[:, None] == pack).astype(jnp.int32), axis=0)
    splits = jnp.sum(selector * first_here[None, :], axis=1)
    back = places - starts
    back = back - jnp.where(back >= splits, splits, 0)
    indices = jnp.arange(HD // 2, dtype=F32)
    angles = back.astype(F32)[:, None] * (THETA ** (-2.0 * indices / HD))[None, :]
    cosines, sines = jnp.cos(angles), jnp.sin(angles)
    cosines = jnp.concatenate([cosines, cosines], axis=1)
    sines = jnp.concatenate([-sines, sines], axis=1)

    combined = jnp.concatenate([query_weight, keyval_weight.reshape(keyval_weight.shape[0], -1)], axis=1)
    w_in = lax.all_gather(combined, "z", axis=0, tiled=True)
    block = width // ny
    half = block // 2

    values = hidden_in.astype(F32)
    scale = lax.rsqrt(jnp.mean(values * values, axis=1, keepdims=True) + EPS)
    own = (values * scale * norm_gain).astype(BF)

    def features(step):
        return lax.dynamic_slice_in_dim(own, (y + step) % ny * block, block, axis=1)

    pack_0 = features(0)
    with jax.named_scope("exchange"):
        rest = jnp.concatenate(
            [hop(features(2), "y", 2), hop(features(1), "y", 1), hop(features(-1), "y", -1)], axis=0
        )

    cols = out_weight.shape[1] // 2
    w_low, w_high = out_weight[:, :cols], out_weight[:, cols:]
    mine = jnp.where(core == 0, w_low, w_high)
    other = swap(jnp.where(core == 0, w_high, w_low))
    with jax.named_scope("own"):
        left_0, right_0 = hop(pack_0, "x", 1), hop(pack_0, "x", -1)
        low_0, high_0 = hop(left_0[:, :half], "x", 1), hop(right_0[:, half:], "x", -1)
    rest, left_0, right_0, low_0, high_0, cosines, sines = after(
        rest, left_0, right_0, low_0, high_0, cosines, sines
    )

    rest_other = swap(rest)
    w_both, rest_other = after(jnp.concatenate([mine, other], axis=0), rest_other)
    with jax.named_scope("w_out"):
        w_near = jnp.stack([w_both, hop(w_both, "y", 1), hop(w_both, "y", 2), hop(w_both, "y", 3)])

    with jax.named_scope("rest"):
        left, right = hop(rest, "x", 1), hop(rest, "x", -1)
        low, high = hop(left[:, :half], "x", 1), hop(right[:, half:], "x", -1)
    w_near, left, right = after(w_near, left, right)
    w_out = lax.all_gather(w_near, "z", axis=0, tiled=True)

    with jax.named_scope("rest"):
        near = [rest, left, right]
        near_sums = [multiply([[t] for t in side], w_in) for side in (near, [rest_other, swap(left), swap(right)])]
        (low, high), near_sums, mine = after(
            (low, high), near_sums, (pack_0, left_0, low_0, high_0, right_0)
        )
        far_sums = [multiply([side], w_in) for side in ([low, high], [swap(low), swap(high)])]
    with jax.named_scope("own"):
        mine = jnp.concatenate(
            [mine[0], mine[1], jnp.concatenate(mine[2:4], axis=1), mine[4]], axis=0
        )
        sum_0 = jnp.concatenate([dot(mine, w_in), dot(swap(mine), w_in)], axis=0)

    def whole(i):
        at = slice(i * here, (i + 1) * here)
        return jnp.concatenate(
            [t[at] for n, f in zip(near_sums, far_sums) for t in (n[0], n[1], f[0], n[2])], axis=0
        )

    sum_2, sum_m, sum_p = whole(0), whole(1), whole(2)

    mid = sum_0.shape[1] // 2
    two = sum_2.astype(BF)
    a = hop(two[:, :mid], "y", 1)
    b = hop(two[:, mid:], "y", -1)
    up = jnp.concatenate(
        [(sum_p[:, :mid] + a.astype(F32)).astype(BF), sum_p[:, mid:].astype(BF)], axis=1
    )
    down = jnp.concatenate(
        [sum_m[:, :mid].astype(BF), (sum_m[:, mid:] + b.astype(F32)).astype(BF)], axis=1
    )
    from_m = hop(up, "y", 1)
    from_p = hop(down, "y", -1)

    capacity = 2 * rows // packs
    lanes = jnp.arange(capacity, dtype=jnp.int32)
    slots = jnp.arange(packs, dtype=jnp.int32)
    outgoing = (move_plan[None, :] == ((slots - pack) % packs)[:, None]).astype(jnp.int32)
    send_start = jnp.sum(outgoing * offsets[None, :], axis=1)
    send_length = jnp.sum(outgoing * lengths[None, :], axis=1)
    live = lanes[None, :] < send_length[:, None]
    send_rows = jnp.where(live, send_start[:, None] + lanes[None, :], -1).reshape(-1)
    bias = jnp.concatenate([query_bias, keyval_bias.reshape(-1)])[None, :]
    sent = attend(
        here,
        q_cols // HD,
        packs * capacity,
        core.reshape(1),
        sum_0,
        from_m,
        from_p,
        bias,
        cosines,
        sines,
        back[:, None],
        places[None, :],
        send_rows[:, None],
    ).reshape(packs, capacity, q_cols)
    got = lax.all_to_all(sent, DP, split_axis=0, concat_axis=0, tiled=True)
    sources = (pack - move_plan) % packs
    bundle_out = jnp.sum((places_out[:, None] >= offsets[None, :]).astype(jnp.int32), axis=1) - 1
    selector = (bundle_out[:, None] == ids[None, :]).astype(jnp.int32)
    source = jnp.sum(selector * sources[None, :], axis=1)
    slot = source * capacity + places_out - jnp.sum(selector * offsets[None, :], axis=1)
    place = (slot[:, None] == jnp.arange(packs * capacity, dtype=jnp.int32)[None, :]).astype(BF)
    moved = dot(place, got.reshape(packs * capacity, q_cols)).astype(BF)
    theirs = swap(moved)

    parts = []
    pair = 2 * here
    chunks = 2
    count = packs // chunks
    for j in range(chunks):
        partial = project_out(j * count, count, moved, theirs, w_out)
        part = [partial[s * pair : (s + 1) * pair] for s in range(4)]
        mid = part[0].shape[1] // 2
        a = hop(part[2][:, :mid], "x", 1)
        b = hop(part[2][:, mid:], "x", -1)
        up = jnp.concatenate(
            [(part[3][:, :mid].astype(F32) + a.astype(F32)).astype(BF), part[3][:, mid:]], axis=1
        )
        down = jnp.concatenate(
            [part[1][:, :mid], (part[1][:, mid:].astype(F32) + b.astype(F32)).astype(BF)], axis=1
        )
        u, v = hop(up, "x", 1), hop(down, "x", -1)
        total = (part[0].astype(F32) + u.astype(F32) + v.astype(F32)).astype(BF)
        parts.append(jnp.where(core == 0, total[:here], total[here:]))
        parts.append(swap(jnp.where(core == 0, total[here:], total[:here])))
    return interleave(ny, cols, jnp.stack([core, y]), parts)


def solution(mesh):
    packs, tensor = mesh.devices.shape
    side = int(round(packs**0.5))
    fine = Mesh(mesh.devices.reshape(side, packs // side, tensor // 2, 2), ("y", "z", "x", "c"))
    every = ("y", "z", "x", "c")
    heads = ("x", "c")
    in_specs = (
        P(every, None),
        P(),
        P(DP, heads),
        P(DP, None, heads),
        P(heads),
        P(None, heads),
        P(heads, DP),
        P(),
        P(),
        P(),
    )
    return jax.shard_map(
        shards, mesh=fine, in_specs=in_specs, out_specs=P(every, None), check_vma=False
    )
```

```python
import functools

import jax
import jax.numpy as jnp
from jax import lax
from jax.experimental import pallas as pl
from jax.experimental.pallas import tpu as pltpu
from jax.sharding import Mesh, PartitionSpec as P

HD = 128
THETA = 1000000.0
EPS = 1e-06
BF = jnp.bfloat16
F32 = jnp.float32
DP = ("y", "z")


def ring(n, step):
    return [(i, (i + step) % n) for i in range(n)]


def hop(v, axis, step):
    with jax.named_scope(f"{axis}{step % lax.axis_size(axis)}"):
        return lax.ppermute(v, axis, ring(lax.axis_size(axis), step))


def swap(v):
    with jax.named_scope("core"):
        return lax.ppermute(v, "c", [(0, 1), (1, 0)])


def after(*values):
    return lax.optimization_barrier(values)


def dot(a, b):
    return jnp.dot(a, b, preferred_element_type=F32)


def attend_kernel(here, heads, core_ref, sum_ref, m_ref, p_ref, bias_ref, cos_ref, sin_ref, back_ref,
                  place_ref, send_ref, out_ref, proj, keys, vals, context):
    rows = sum_ref.shape[0]
    q_cols = heads * HD
    proj[...] = sum_ref[...] + m_ref[...].astype(F32) + p_ref[...].astype(F32) + bias_ref[...]

    def turned(u, at):
        swapped = jnp.concatenate([u[:, HD // 2 :], u[:, : HD // 2]], axis=1)
        return u * cos_ref[at, :] + swapped * sin_ref[at, :]

    every = pl.ds(0, rows)
    keys[...] = turned(proj[:, q_cols : q_cols + HD], every).astype(BF).astype(F32)
    vals[...] = proj[:, q_cols + HD :].astype(BF).astype(F32)
    core = core_ref[0]
    chips = rows // (2 * here)
    lane = lax.broadcasted_iota(jnp.int32, (here, 2 * here), 1)
    own = here + lax.broadcasted_iota(jnp.int32, (here, 2 * here), 0)
    for k in range(2):
        c = core if k == 0 else 1 - core
        for s in range(chips):
            at = pl.ds((k * chips + s) * here, here)
            before = pl.ds(pl.multiple_of(((1 - k) * chips + lax.rem(s + 1 - c, chips)) * here, 8), here)
            ks = jnp.concatenate([keys[before, :], keys[at, :]], axis=0).astype(BF)
            vs = jnp.concatenate([vals[before, :], vals[at, :]], axis=0).astype(BF)
            q = jnp.concatenate(
                [turned(proj[at, h * HD : (h + 1) * HD], at) for h in range(heads)], axis=0
            ).astype(BF)
            scores = lax.dot_general(q, ks, (((1,), (1,)), ((), ())), preferred_element_type=F32)
            allowed = (lane <= own) & (lane >= own - back_ref[at, :])
            allowed = jnp.concatenate([allowed.astype(jnp.int32)] * heads, axis=0) > 0
            scores = jnp.where(allowed, scores * HD ** (-0.5), -jnp.inf)
            e = jnp.exp(scores - jnp.max(scores, axis=1, keepdims=True))
            probs = (e / jnp.sum(e, axis=1, keepdims=True)).astype(BF)
            ctx = jnp.dot(probs, vs, preferred_element_type=F32)
            for h in range(heads):
                context[at, h * HD : (h + 1) * HD] = ctx[h * here : (h + 1) * here]
    ctx = context[...].astype(BF)
    step = out_ref.shape[0] // 4
    for i in range(4):
        at = pl.ds(i * step, step)
        pick = jnp.where(send_ref[at, :] == place_ref[...], 1.0, 0.0).astype(BF)
        out_ref[at, :] = jnp.dot(pick, ctx, preferred_element_type=F32).astype(BF)


def attend(here, heads, slots, core, total, part_m, part_p, bias, cosines, sines, back, places, send_rows):
    rows, cols = total.shape
    vmem = pl.BlockSpec(memory_space=pltpu.VMEM)
    return pl.pallas_call(
        functools.partial(attend_kernel, here, heads),
        out_shape=jax.ShapeDtypeStruct((slots, heads * HD), BF),
        in_specs=[pl.BlockSpec(memory_space=pltpu.SMEM)] + [vmem] * 9,
        out_specs=vmem,
        scratch_shapes=[
            pltpu.VMEM((rows, cols), F32),
            pltpu.VMEM((rows, HD), F32),
            pltpu.VMEM((rows, HD), F32),
            pltpu.VMEM((rows, heads * HD), F32),
        ],
        compiler_params=pltpu.CompilerParams(vmem_limit_bytes=40 * 1024 * 1024),
        cost_estimate=pl.CostEstimate(flops=1 << 30, bytes_accessed=8 << 20, transcendentals=1 << 20),
    )(core, total, part_m, part_p, bias, cosines, sines, back, places, send_rows)


def multiply_kernel(sizes, w_ref, *refs):
    at = 0
    outs = refs[sum(sizes) :]
    for count, out_ref in zip(sizes, outs):
        total, depth = 0.0, 0
        for ref in refs[at : at + count]:
            total += jnp.dot(
                ref[...], w_ref[depth : depth + ref.shape[1]], preferred_element_type=F32
            )
            depth += ref.shape[1]
        out_ref[...] = total
        at += count


def multiply(products, w):
    flat = [t for pieces in products for t in pieces]
    vmem = pl.BlockSpec(memory_space=pltpu.VMEM)
    return pl.pallas_call(
        functools.partial(multiply_kernel, [len(pieces) for pieces in products]),
        out_shape=[jax.ShapeDtypeStruct((p[0].shape[0], w.shape[1]), F32) for p in products],
        in_specs=[vmem] * (1 + len(flat)),
        out_specs=[vmem] * len(products),
        compiler_params=pltpu.CompilerParams(vmem_limit_bytes=32 * 1024 * 1024),
        cost_estimate=pl.CostEstimate(flops=1 << 20, bytes_accessed=1 << 12, transcendentals=0),
    )(w, *flat)


def project_out_kernel(mine_ref, theirs_ref, w_ref, out_ref):
    both = jnp.concatenate([mine_ref[...], theirs_ref[...]], axis=1)
    w = jnp.concatenate([w_ref[i] for i in range(w_ref.shape[0])], axis=1)
    out_ref[...] = jnp.dot(both, w, preferred_element_type=F32).astype(BF)


def project_out(first, count, mine, theirs, w):
    rows, depth = mine.shape
    _, deep, width = w.shape
    group = 2
    whole = pl.BlockSpec((rows, depth), lambda d: (0, 0))
    return pl.pallas_call(
        project_out_kernel,
        out_shape=jax.ShapeDtypeStruct((rows, count * width), BF),
        grid=(count // group,),
        in_specs=[whole, whole, pl.BlockSpec((group, deep, width), lambda d: (first // group + d, 0, 0))],
        out_specs=pl.BlockSpec((rows, group * width), lambda d: (0, d)),
        compiler_params=pltpu.CompilerParams(vmem_limit_bytes=48 * 1024 * 1024),
        cost_estimate=pl.CostEstimate(
            flops=2 * rows * deep * width * count, bytes_accessed=8 << 20, transcendentals=0
        ),
    )(mine, theirs, w)


def interleave_kernel(side, width, at_ref, *refs):
    *parts, out_ref = refs
    core, y = at_ref[0], at_ref[1]
    blocks = parts[0].shape[1] // width
    for j in range(len(parts) // 2):
        for i in range(blocks):
            z, back = divmod(j * blocks + i, side)
            at = lax.rem(y + side - back, side) * side + z
            for part, c in ((parts[2 * j], core), (parts[2 * j + 1], 1 - core)):
                to = pl.multiple_of((at * 2 + c) * width, width)
                out_ref[:, pl.ds(to, width)] = part[:, i * width : (i + 1) * width]


def interleave(side, width, at, parts):
    rows, cols = parts[0].shape
    vmem = pl.BlockSpec(memory_space=pltpu.VMEM)
    return pl.pallas_call(
        functools.partial(interleave_kernel, side, width),
        out_shape=jax.ShapeDtypeStruct((rows, cols * len(parts)), BF),
        in_specs=[pl.BlockSpec(memory_space=pltpu.SMEM)] + [vmem] * len(parts),
        out_specs=vmem,
    )(at, *parts)


def shards(
    hidden_in,
    norm_gain,
    query_weight,
    keyval_weight,
    query_bias,
    keyval_bias,
    out_weight,
    lengths,
    move_plan,
    first_len,
):
    packs = lax.axis_size(DP)
    pack = lax.axis_index(DP)
    x = lax.axis_index("x")
    y = lax.axis_index("y")
    core = lax.axis_index("c")
    nx = lax.axis_size("x")
    ny = lax.axis_size("y")
    z = lax.axis_index("z")
    nz = lax.axis_size("z")
    here = hidden_in.shape[0]
    width = hidden_in.shape[1]
    rows = here * nx * 2
    q_cols = query_weight.shape[1]

    r = jnp.arange(here, dtype=jnp.int32)
    places = jnp.concatenate(
        [
            here * (2 * ((x - s) % nx) + (core if k == 0 else 1 - core)) + r
            for k in range(2)
            for s in range(4)
        ]
    )
    places_out = jnp.concatenate(
        [here * (2 * ((x - s) % nx) + k) + r for s in range(4) for k in range(2)]
    )

    ids = jnp.arange(lengths.shape[0], dtype=jnp.int32)
    offsets = jnp.cumsum(lengths) - lengths
    bundle = jnp.sum((places[:, None] >= offsets[None, :]).astype(jnp.int32), axis=1) - 1
    selector = (bundle[:, None] == ids[None, :]).astype(jnp.int32)
    starts = jnp.sum(selector * offsets[None, :], axis=1)
    first_here = jnp.sum(first_len * (jnp.arange(packs)[:, None] == pack).astype(jnp.int32), axis=0)
    splits = jnp.sum(selector * first_here[None, :], axis=1)
    back = places - starts
    back = back - jnp.where(back >= splits, splits, 0)
    indices = jnp.arange(HD // 2, dtype=F32)
    angles = back.astype(F32)[:, None] * (THETA ** (-2.0 * indices / HD))[None, :]
    cosines, sines = jnp.cos(angles), jnp.sin(angles)
    cosines = jnp.concatenate([cosines, cosines], axis=1)
    sines = jnp.concatenate([-sines, sines], axis=1)

    combined = jnp.concatenate([query_weight, keyval_weight.reshape(keyval_weight.shape[0], -1)], axis=1)
    hidden_in, combined = after(hidden_in, combined)
    w_in = lax.all_gather(combined, "z", axis=0, tiled=True)
    block = width // ny
    half = block // 2

    values = hidden_in.astype(F32)
    scale = lax.rsqrt(jnp.mean(values * values, axis=1, keepdims=True) + EPS)
    own = (values * scale * norm_gain).astype(BF)

    def features(step):
        return lax.dynamic_slice_in_dim(own, (y + step) % ny * block, block, axis=1)

    pack_0 = features(0)
    with jax.named_scope("exchange"):
        rest = jnp.concatenate(
            [hop(features(2), "y", 2), hop(features(1), "y", 1), hop(features(-1), "y", -1)], axis=0
        )

    cols = out_weight.shape[1] // 2
    w_low, w_high = out_weight[:, :cols], out_weight[:, cols:]
    mine = jnp.where(core == 0, w_low, w_high)
    other = swap(jnp.where(core == 0, w_high, w_low))
    with jax.named_scope("own"):
        left_0, right_0 = hop(pack_0, "x", 1), hop(pack_0, "x", -1)
        low_0, high_0 = hop(left_0[:, :half], "x", 1), hop(right_0[:, half:], "x", -1)
    w_both = jnp.concatenate([mine, other], axis=0)
    rest, left_0, right_0, low_0, high_0, cosines, sines, w_both = after(
        rest, left_0, right_0, low_0, high_0, cosines, sines, w_both
    )

    rest_other = swap(rest)
    with jax.named_scope("w_out"):
        w_near = jnp.stack([w_both, hop(w_both, "y", 1), hop(w_both, "y", 2), hop(w_both, "y", 3)])

    with jax.named_scope("rest"):
        left, right = hop(rest, "x", 1), hop(rest, "x", -1)
        low, high = hop(left[:, :half], "x", 1), hop(right[:, half:], "x", -1)
    w_near, left, right = after(w_near, left, right)
    w_out = lax.all_gather(w_near, "z", axis=0, tiled=True)

    with jax.named_scope("rest"):
        near = [rest, left, right]
        near_sums = [multiply([[t] for t in side], w_in) for side in (near, [rest_other, swap(left), swap(right)])]
        (low, high), near_sums, mine = after(
            (low, high), near_sums, (pack_0, left_0, low_0, high_0, right_0)
        )
        far_sums = [multiply([side], w_in) for side in ([low, high], [swap(low), swap(high)])]
    with jax.named_scope("own"):
        mine = jnp.concatenate(
            [mine[0], mine[1], jnp.concatenate(mine[2:4], axis=1), mine[4]], axis=0
        )
        sum_0 = jnp.concatenate([dot(mine, w_in), dot(swap(mine), w_in)], axis=0)

    def whole(i):
        at = slice(i * here, (i + 1) * here)
        return jnp.concatenate(
            [t[at] for n, f in zip(near_sums, far_sums) for t in (n[0], n[1], f[0], n[2])], axis=0
        )

    sum_2, sum_m, sum_p = whole(0), whole(1), whole(2)

    mid = sum_0.shape[1] // 2
    two = sum_2.astype(BF)
    a = hop(two[:, :mid], "y", 1)
    b = hop(two[:, mid:], "y", -1)
    up = jnp.concatenate(
        [(sum_p[:, :mid] + a.astype(F32)).astype(BF), sum_p[:, mid:].astype(BF)], axis=1
    )
    down = jnp.concatenate(
        [sum_m[:, :mid].astype(BF), (sum_m[:, mid:] + b.astype(F32)).astype(BF)], axis=1
    )
    from_m = hop(up, "y", 1)
    from_p = hop(down, "y", -1)

    capacity = 2 * rows // packs
    lanes = jnp.arange(capacity, dtype=jnp.int32)
    slots = jnp.arange(packs, dtype=jnp.int32)
    outgoing = (move_plan[None, :] == ((slots - pack) % packs)[:, None]).astype(jnp.int32)
    send_start = jnp.sum(outgoing * offsets[None, :], axis=1)
    send_length = jnp.sum(outgoing * lengths[None, :], axis=1)
    live = lanes[None, :] < send_length[:, None]
    send_rows = jnp.where(live, send_start[:, None] + lanes[None, :], -1).reshape(-1)
    bias = jnp.concatenate([query_bias, keyval_bias.reshape(-1)])[None, :]
    sent = attend(
        here,
        q_cols // HD,
        packs * capacity,
        core.reshape(1),
        sum_0,
        from_m,
        from_p,
        bias,
        cosines,
        sines,
        back[:, None],
        places[None, :],
        send_rows[:, None],
    ).reshape(packs, capacity, q_cols)
    got = lax.all_to_all(sent, DP, split_axis=0, concat_axis=0, tiled=True)
    sources = (pack - move_plan) % packs
    bundle_out = jnp.sum((places_out[:, None] >= offsets[None, :]).astype(jnp.int32), axis=1) - 1
    selector = (bundle_out[:, None] == ids[None, :]).astype(jnp.int32)
    source = jnp.sum(selector * sources[None, :], axis=1)
    slot = source * capacity + places_out - jnp.sum(selector * offsets[None, :], axis=1)
    place = (slot[:, None] == jnp.arange(packs * capacity, dtype=jnp.int32)[None, :]).astype(BF)
    moved = dot(place, got.reshape(packs * capacity, q_cols)).astype(BF)
    theirs = swap(moved)

    parts = []
    pair = 2 * here
    chunks = 2
    count = packs // chunks
    for j in range(chunks):
        partial = project_out(j * count, count, moved, theirs, w_out)
        part = [partial[s * pair : (s + 1) * pair] for s in range(4)]
        mid = part[0].shape[1] // 2
        a = hop(part[2][:, :mid], "x", 1)
        b = hop(part[2][:, mid:], "x", -1)
        up = jnp.concatenate(
            [(part[3][:, :mid].astype(F32) + a.astype(F32)).astype(BF), part[3][:, mid:]], axis=1
        )
        down = jnp.concatenate(
            [part[1][:, :mid], (part[1][:, mid:].astype(F32) + b.astype(F32)).astype(BF)], axis=1
        )
        u, v = hop(up, "x", 1), hop(down, "x", -1)
        total = (part[0].astype(F32) + u.astype(F32) + v.astype(F32)).astype(BF)
        parts.append(jnp.where(core == 0, total[:here], total[here:]))
        parts.append(swap(jnp.where(core == 0, total[here:], total[:here])))
    return interleave(ny, cols, jnp.stack([core, y]), parts)


def solution(mesh):
    packs, tensor = mesh.devices.shape
    side = int(round(packs**0.5))
    fine = Mesh(mesh.devices.reshape(side, packs // side, tensor // 2, 2), ("y", "z", "x", "c"))
    every = ("y", "z", "x", "c")
    heads = ("x", "c")
    in_specs = (
        P(every, None),
        P(),
        P(DP, heads),
        P(DP, None, heads),
        P(heads),
        P(None, heads),
        P(heads, DP),
        P(),
        P(),
        P(),
    )
    return jax.shard_map(
        shards, mesh=fine, in_specs=in_specs, out_specs=P(every, None), check_vma=False
    )
```

```python
import functools

import jax
import jax.numpy as jnp
from jax import lax
from jax.experimental import pallas as pl
from jax.experimental.pallas import tpu as pltpu
from jax.sharding import Mesh, PartitionSpec as P

HD = 128
THETA = 1000000.0
EPS = 1e-06
BF = jnp.bfloat16
F32 = jnp.float32
DP = ("y", "z")


def ring(n, step):
    return [(i, (i + step) % n) for i in range(n)]


def hop(v, axis, step):
    with jax.named_scope(f"{axis}{step % lax.axis_size(axis)}"):
        return lax.ppermute(v, axis, ring(lax.axis_size(axis), step))


def swap(v):
    with jax.named_scope("core"):
        return lax.ppermute(v, "c", [(0, 1), (1, 0)])


def after(*values):
    return lax.optimization_barrier(values)


def dot(a, b):
    return jnp.dot(a, b, preferred_element_type=F32)


def attend_kernel(here, heads, core_ref, sum_ref, m_ref, p_ref, bias_ref, cos_ref, sin_ref, back_ref,
                  place_ref, send_ref, out_ref, proj, keys, vals, context):
    rows = sum_ref.shape[0]
    q_cols = heads * HD
    proj[...] = sum_ref[...] + m_ref[...].astype(F32) + p_ref[...].astype(F32) + bias_ref[...]

    def turned(u, at):
        swapped = jnp.concatenate([u[:, HD // 2 :], u[:, : HD // 2]], axis=1)
        return u * cos_ref[at, :] + swapped * sin_ref[at, :]

    every = pl.ds(0, rows)
    keys[...] = turned(proj[:, q_cols : q_cols + HD], every).astype(BF).astype(F32)
    vals[...] = proj[:, q_cols + HD :].astype(BF).astype(F32)
    core = core_ref[0]
    chips = rows // (2 * here)
    lane = lax.broadcasted_iota(jnp.int32, (here, 2 * here), 1)
    own = here + lax.broadcasted_iota(jnp.int32, (here, 2 * here), 0)
    for k in range(2):
        c = core if k == 0 else 1 - core
        for s in range(chips):
            at = pl.ds((k * chips + s) * here, here)
            before = pl.ds(pl.multiple_of(((1 - k) * chips + lax.rem(s + 1 - c, chips)) * here, 8), here)
            ks = jnp.concatenate([keys[before, :], keys[at, :]], axis=0).astype(BF)
            vs = jnp.concatenate([vals[before, :], vals[at, :]], axis=0).astype(BF)
            q = jnp.concatenate(
                [turned(proj[at, h * HD : (h + 1) * HD], at) for h in range(heads)], axis=0
            ).astype(BF)
            scores = lax.dot_general(q, ks, (((1,), (1,)), ((), ())), preferred_element_type=F32)
            allowed = (lane <= own) & (lane >= own - back_ref[at, :])
            allowed = jnp.concatenate([allowed.astype(jnp.int32)] * heads, axis=0) > 0
            scores = jnp.where(allowed, scores * HD ** (-0.5), -jnp.inf)
            e = jnp.exp(scores - jnp.max(scores, axis=1, keepdims=True))
            probs = (e / jnp.sum(e, axis=1, keepdims=True)).astype(BF)
            ctx = jnp.dot(probs, vs, preferred_element_type=F32)
            for h in range(heads):
                context[at, h * HD : (h + 1) * HD] = ctx[h * here : (h + 1) * here]
    ctx = context[...].astype(BF)
    step = out_ref.shape[0] // 4
    for i in range(4):
        at = pl.ds(i * step, step)
        pick = jnp.where(send_ref[at, :] == place_ref[...], 1.0, 0.0).astype(BF)
        out_ref[at, :] = jnp.dot(pick, ctx, preferred_element_type=F32).astype(BF)


def attend(here, heads, slots, core, total, part_m, part_p, bias, cosines, sines, back, places, send_rows):
    rows, cols = total.shape
    vmem = pl.BlockSpec(memory_space=pltpu.VMEM)
    return pl.pallas_call(
        functools.partial(attend_kernel, here, heads),
        out_shape=jax.ShapeDtypeStruct((slots, heads * HD), BF),
        in_specs=[pl.BlockSpec(memory_space=pltpu.SMEM)] + [vmem] * 9,
        out_specs=vmem,
        scratch_shapes=[
            pltpu.VMEM((rows, cols), F32),
            pltpu.VMEM((rows, HD), F32),
            pltpu.VMEM((rows, HD), F32),
            pltpu.VMEM((rows, heads * HD), F32),
        ],
        compiler_params=pltpu.CompilerParams(vmem_limit_bytes=40 * 1024 * 1024),
        cost_estimate=pl.CostEstimate(flops=1 << 30, bytes_accessed=8 << 20, transcendentals=1 << 20),
    )(core, total, part_m, part_p, bias, cosines, sines, back, places, send_rows)


def multiply_kernel(sizes, w_ref, *refs):
    at = 0
    outs = refs[sum(sizes) :]
    for count, out_ref in zip(sizes, outs):
        total, depth = 0.0, 0
        for ref in refs[at : at + count]:
            total += jnp.dot(
                ref[...], w_ref[depth : depth + ref.shape[1]], preferred_element_type=F32
            )
            depth += ref.shape[1]
        out_ref[...] = total
        at += count


def multiply(products, w):
    flat = [t for pieces in products for t in pieces]
    vmem = pl.BlockSpec(memory_space=pltpu.VMEM)
    return pl.pallas_call(
        functools.partial(multiply_kernel, [len(pieces) for pieces in products]),
        out_shape=[jax.ShapeDtypeStruct((p[0].shape[0], w.shape[1]), F32) for p in products],
        in_specs=[vmem] * (1 + len(flat)),
        out_specs=[vmem] * len(products),
        compiler_params=pltpu.CompilerParams(vmem_limit_bytes=32 * 1024 * 1024),
        cost_estimate=pl.CostEstimate(flops=1 << 20, bytes_accessed=1 << 12, transcendentals=0),
    )(w, *flat)


def project_out_kernel(mine_ref, theirs_ref, w_ref, out_ref):
    both = jnp.concatenate([mine_ref[...], theirs_ref[...]], axis=1)
    w = jnp.concatenate([w_ref[i] for i in range(w_ref.shape[0])], axis=1)
    out_ref[...] = jnp.dot(both, w, preferred_element_type=F32).astype(BF)


def project_out(first, count, mine, theirs, w):
    rows, depth = mine.shape
    _, deep, width = w.shape
    group = 2
    whole = pl.BlockSpec((rows, depth), lambda d: (0, 0))
    return pl.pallas_call(
        project_out_kernel,
        out_shape=jax.ShapeDtypeStruct((rows, count * width), BF),
        grid=(count // group,),
        in_specs=[whole, whole, pl.BlockSpec((group, deep, width), lambda d: (first // group + d, 0, 0))],
        out_specs=pl.BlockSpec((rows, group * width), lambda d: (0, d)),
        compiler_params=pltpu.CompilerParams(vmem_limit_bytes=48 * 1024 * 1024),
        cost_estimate=pl.CostEstimate(
            flops=2 * rows * deep * width * count, bytes_accessed=8 << 20, transcendentals=0
        ),
    )(mine, theirs, w)


def interleave_kernel(side, width, at_ref, *refs):
    *parts, out_ref = refs
    core, y = at_ref[0], at_ref[1]
    blocks = parts[0].shape[1] // width
    for j in range(len(parts) // 2):
        for i in range(blocks):
            z, back = divmod(j * blocks + i, side)
            at = lax.rem(y + side - back, side) * side + z
            for part, c in ((parts[2 * j], core), (parts[2 * j + 1], 1 - core)):
                to = pl.multiple_of((at * 2 + c) * width, width)
                out_ref[:, pl.ds(to, width)] = part[:, i * width : (i + 1) * width]


def interleave(side, width, at, parts):
    rows, cols = parts[0].shape
    vmem = pl.BlockSpec(memory_space=pltpu.VMEM)
    return pl.pallas_call(
        functools.partial(interleave_kernel, side, width),
        out_shape=jax.ShapeDtypeStruct((rows, cols * len(parts)), BF),
        in_specs=[pl.BlockSpec(memory_space=pltpu.SMEM)] + [vmem] * len(parts),
        out_specs=vmem,
    )(at, *parts)


def shards(
    hidden_in,
    norm_gain,
    query_weight,
    keyval_weight,
    query_bias,
    keyval_bias,
    out_weight,
    lengths,
    move_plan,
    first_len,
):
    packs = lax.axis_size(DP)
    pack = lax.axis_index(DP)
    x = lax.axis_index("x")
    y = lax.axis_index("y")
    core = lax.axis_index("c")
    nx = lax.axis_size("x")
    ny = lax.axis_size("y")
    z = lax.axis_index("z")
    nz = lax.axis_size("z")
    here = hidden_in.shape[0]
    width = hidden_in.shape[1]
    rows = here * nx * 2
    q_cols = query_weight.shape[1]

    r = jnp.arange(here, dtype=jnp.int32)
    places = jnp.concatenate(
        [
            here * (2 * ((x - s) % nx) + (core if k == 0 else 1 - core)) + r
            for k in range(2)
            for s in range(4)
        ]
    )
    places_out = jnp.concatenate(
        [here * (2 * ((x - s) % nx) + k) + r for s in range(4) for k in range(2)]
    )

    ids = jnp.arange(lengths.shape[0], dtype=jnp.int32)
    offsets = jnp.cumsum(lengths) - lengths
    bundle = jnp.sum((places[:, None] >= offsets[None, :]).astype(jnp.int32), axis=1) - 1
    selector = (bundle[:, None] == ids[None, :]).astype(jnp.int32)
    starts = jnp.sum(selector * offsets[None, :], axis=1)
    first_here = jnp.sum(first_len * (jnp.arange(packs)[:, None] == pack).astype(jnp.int32), axis=0)
    splits = jnp.sum(selector * first_here[None, :], axis=1)
    back = places - starts
    back = back - jnp.where(back >= splits, splits, 0)
    indices = jnp.arange(HD // 2, dtype=F32)
    angles = back.astype(F32)[:, None] * (THETA ** (-2.0 * indices / HD))[None, :]
    cosines, sines = jnp.cos(angles), jnp.sin(angles)
    cosines = jnp.concatenate([cosines, cosines], axis=1)
    sines = jnp.concatenate([-sines, sines], axis=1)

    combined = jnp.concatenate([query_weight, keyval_weight.reshape(keyval_weight.shape[0], -1)], axis=1)
    hidden_in, combined = after(hidden_in, combined)
    w_in = lax.all_gather(combined, "z", axis=0, tiled=True)
    block = width // ny
    half = block // 2

    values = hidden_in.astype(F32)
    scale = lax.rsqrt(jnp.mean(values * values, axis=1, keepdims=True) + EPS)
    own = (values * scale * norm_gain).astype(BF)

    def features(step):
        return lax.dynamic_slice_in_dim(own, (y + step) % ny * block, block, axis=1)

    pack_0 = features(0)
    with jax.named_scope("exchange"):
        rest = jnp.concatenate(
            [hop(features(2), "y", 2), hop(features(1), "y", 1), hop(features(-1), "y", -1)], axis=0
        )

    cols = out_weight.shape[1] // 2
    w_low, w_high = out_weight[:, :cols], out_weight[:, cols:]
    mine = jnp.where(core == 0, w_low, w_high)
    other = swap(jnp.where(core == 0, w_high, w_low))
    with jax.named_scope("own"):
        left_0, right_0 = hop(pack_0, "x", 1), hop(pack_0, "x", -1)
        low_0, high_0 = hop(left_0[:, :half], "x", 1), hop(right_0[:, half:], "x", -1)
    w_both = jnp.concatenate([mine, other], axis=0)
    rest, left_0, right_0, low_0, high_0, cosines, sines, w_both = after(
        rest, left_0, right_0, low_0, high_0, cosines, sines, w_both
    )

    rest_other = swap(rest)
    with jax.named_scope("w_out"):
        w_near = [w_both] + [hop(w_both, "y", i) for i in range(1, ny)]

    with jax.named_scope("rest"):
        left, right = hop(rest, "x", 1), hop(rest, "x", -1)
        low, high = hop(left[:, :half], "x", 1), hop(right[:, half:], "x", -1)
    w_near, low, high, left_in, right_in = after(w_near, low, high, left, right)
    w_out = lax.all_gather(jnp.stack(w_near), "z", axis=0, tiled=True)

    with jax.named_scope("rest"):
        near = [rest, left, right]
        near_sums = [multiply([[t] for t in side], w_in) for side in (near, [rest_other, swap(left_in), swap(right_in)])]
        (low, high), near_sums, mine = after(
            (low, high), near_sums, (pack_0, left_0, low_0, high_0, right_0)
        )
        far_sums = [multiply([side], w_in) for side in ([low, high], [swap(low), swap(high)])]
    with jax.named_scope("own"):
        mine = jnp.concatenate(
            [mine[0], mine[1], jnp.concatenate(mine[2:4], axis=1), mine[4]], axis=0
        )
        sum_0 = jnp.concatenate([dot(mine, w_in), dot(swap(mine), w_in)], axis=0)

    def whole(i):
        at = slice(i * here, (i + 1) * here)
        return jnp.concatenate(
            [t[at] for n, f in zip(near_sums, far_sums) for t in (n[0], n[1], f[0], n[2])], axis=0
        )

    sum_2, sum_m, sum_p = whole(0), whole(1), whole(2)

    mid = sum_0.shape[1] // 2
    two = sum_2.astype(BF)
    a = hop(two[:, :mid], "y", 1)
    b = hop(two[:, mid:], "y", -1)
    up = jnp.concatenate(
        [(sum_p[:, :mid] + a.astype(F32)).astype(BF), sum_p[:, mid:].astype(BF)], axis=1
    )
    down = jnp.concatenate(
        [sum_m[:, :mid].astype(BF), (sum_m[:, mid:] + b.astype(F32)).astype(BF)], axis=1
    )
    from_m = hop(up, "y", 1)
    from_p = hop(down, "y", -1)

    capacity = 2 * rows // packs
    lanes = jnp.arange(capacity, dtype=jnp.int32)
    slots = jnp.arange(packs, dtype=jnp.int32)
    outgoing = (move_plan[None, :] == ((slots - pack) % packs)[:, None]).astype(jnp.int32)
    send_start = jnp.sum(outgoing * offsets[None, :], axis=1)
    send_length = jnp.sum(outgoing * lengths[None, :], axis=1)
    live = lanes[None, :] < send_length[:, None]
    send_rows = jnp.where(live, send_start[:, None] + lanes[None, :], -1).reshape(-1)
    bias = jnp.concatenate([query_bias, keyval_bias.reshape(-1)])[None, :]
    sent = attend(
        here,
        q_cols // HD,
        packs * capacity,
        core.reshape(1),
        sum_0,
        from_m,
        from_p,
        bias,
        cosines,
        sines,
        back[:, None],
        places[None, :],
        send_rows[:, None],
    ).reshape(packs, capacity, q_cols)
    got = lax.all_to_all(sent, DP, split_axis=0, concat_axis=0, tiled=True)
    sources = (pack - move_plan) % packs
    bundle_out = jnp.sum((places_out[:, None] >= offsets[None, :]).astype(jnp.int32), axis=1) - 1
    selector = (bundle_out[:, None] == ids[None, :]).astype(jnp.int32)
    source = jnp.sum(selector * sources[None, :], axis=1)
    slot = source * capacity + places_out - jnp.sum(selector * offsets[None, :], axis=1)
    place = (slot[:, None] == jnp.arange(packs * capacity, dtype=jnp.int32)[None, :]).astype(BF)
    moved = dot(place, got.reshape(packs * capacity, q_cols)).astype(BF)
    theirs = swap(moved)

    parts = []
    pair = 2 * here
    chunks = 2
    count = packs // chunks
    for j in range(chunks):
        partial = project_out(j * count, count, moved, theirs, w_out)
        part = [partial[s * pair : (s + 1) * pair] for s in range(4)]
        mid = part[0].shape[1] // 2
        a = hop(part[2][:, :mid], "x", 1)
        b = hop(part[2][:, mid:], "x", -1)
        up = jnp.concatenate(
            [(part[3][:, :mid].astype(F32) + a.astype(F32)).astype(BF), part[3][:, mid:]], axis=1
        )
        down = jnp.concatenate(
            [part[1][:, :mid], (part[1][:, mid:].astype(F32) + b.astype(F32)).astype(BF)], axis=1
        )
        u, v = hop(up, "x", 1), hop(down, "x", -1)
        total = (part[0].astype(F32) + u.astype(F32) + v.astype(F32)).astype(BF)
        parts.append(jnp.where(core == 0, total[:here], total[here:]))
        parts.append(swap(jnp.where(core == 0, total[here:], total[:here])))
    return interleave(ny, cols, jnp.stack([core, y]), parts)


def solution(mesh):
    packs, tensor = mesh.devices.shape
    side = int(round(packs**0.5))
    fine = Mesh(mesh.devices.reshape(side, packs // side, tensor // 2, 2), ("y", "z", "x", "c"))
    every = ("y", "z", "x", "c")
    heads = ("x", "c")
    in_specs = (
        P(every, None),
        P(),
        P(DP, heads),
        P(DP, None, heads),
        P(heads),
        P(None, heads),
        P(heads, DP),
        P(),
        P(),
        P(),
    )
    return jax.shard_map(
        shards, mesh=fine, in_specs=in_specs, out_specs=P(every, None), check_vma=False
    )
```

```python
import functools

import jax
import jax.numpy as jnp
from jax import lax
from jax.experimental import pallas as pl
from jax.experimental.pallas import tpu as pltpu
from jax.sharding import Mesh, PartitionSpec as P

HD = 128
THETA = 1000000.0
EPS = 1e-06
BF = jnp.bfloat16
F32 = jnp.float32
DP = ("y", "z")


def ring(n, step):
    return [(i, (i + step) % n) for i in range(n)]


def hop(v, axis, step):
    with jax.named_scope(f"{axis}{step % lax.axis_size(axis)}"):
        return lax.ppermute(v, axis, ring(lax.axis_size(axis), step))


def swap(v):
    with jax.named_scope("core"):
        return lax.ppermute(v, "c", [(0, 1), (1, 0)])


def after(*values):
    return lax.optimization_barrier(values)


def dot(a, b):
    return jnp.dot(a, b, preferred_element_type=F32)


def attend_kernel(here, heads, core_ref, sum_ref, m_ref, p_ref, bias_ref, cos_ref, sin_ref, back_ref,
                  place_ref, send_ref, out_ref, proj, keys, vals, context):
    rows = sum_ref.shape[0]
    q_cols = heads * HD
    proj[...] = sum_ref[...] + m_ref[...].astype(F32) + p_ref[...].astype(F32) + bias_ref[...]

    def turned(u, at):
        swapped = jnp.concatenate([u[:, HD // 2 :], u[:, : HD // 2]], axis=1)
        return u * cos_ref[at, :] + swapped * sin_ref[at, :]

    every = pl.ds(0, rows)
    keys[...] = turned(proj[:, q_cols : q_cols + HD], every).astype(BF).astype(F32)
    vals[...] = proj[:, q_cols + HD :].astype(BF).astype(F32)
    core = core_ref[0]
    chips = rows // (2 * here)
    lane = lax.broadcasted_iota(jnp.int32, (here, 2 * here), 1)
    own = here + lax.broadcasted_iota(jnp.int32, (here, 2 * here), 0)
    for k in range(2):
        c = core if k == 0 else 1 - core
        for s in range(chips):
            at = pl.ds((k * chips + s) * here, here)
            before = pl.ds(pl.multiple_of(((1 - k) * chips + lax.rem(s + 1 - c, chips)) * here, 8), here)
            ks = jnp.concatenate([keys[before, :], keys[at, :]], axis=0).astype(BF)
            vs = jnp.concatenate([vals[before, :], vals[at, :]], axis=0).astype(BF)
            q = jnp.concatenate(
                [turned(proj[at, h * HD : (h + 1) * HD], at) for h in range(heads)], axis=0
            ).astype(BF)
            scores = lax.dot_general(q, ks, (((1,), (1,)), ((), ())), preferred_element_type=F32)
            allowed = (lane <= own) & (lane >= own - back_ref[at, :])
            allowed = jnp.concatenate([allowed.astype(jnp.int32)] * heads, axis=0) > 0
            scores = jnp.where(allowed, scores * HD ** (-0.5), -jnp.inf)
            e = jnp.exp(scores - jnp.max(scores, axis=1, keepdims=True))
            probs = (e / jnp.sum(e, axis=1, keepdims=True)).astype(BF)
            ctx = jnp.dot(probs, vs, preferred_element_type=F32)
            for h in range(heads):
                context[at, h * HD : (h + 1) * HD] = ctx[h * here : (h + 1) * here]
    ctx = context[...].astype(BF)
    step = out_ref.shape[0] // 4
    for i in range(4):
        at = pl.ds(i * step, step)
        pick = jnp.where(send_ref[at, :] == place_ref[...], 1.0, 0.0).astype(BF)
        out_ref[at, :] = jnp.dot(pick, ctx, preferred_element_type=F32).astype(BF)


def attend(here, heads, slots, core, total, part_m, part_p, bias, cosines, sines, back, places, send_rows):
    rows, cols = total.shape
    vmem = pl.BlockSpec(memory_space=pltpu.VMEM)
    return pl.pallas_call(
        functools.partial(attend_kernel, here, heads),
        out_shape=jax.ShapeDtypeStruct((slots, heads * HD), BF),
        in_specs=[pl.BlockSpec(memory_space=pltpu.SMEM)] + [vmem] * 9,
        out_specs=vmem,
        scratch_shapes=[
            pltpu.VMEM((rows, cols), F32),
            pltpu.VMEM((rows, HD), F32),
            pltpu.VMEM((rows, HD), F32),
            pltpu.VMEM((rows, heads * HD), F32),
        ],
        compiler_params=pltpu.CompilerParams(vmem_limit_bytes=40 * 1024 * 1024),
        cost_estimate=pl.CostEstimate(flops=1 << 30, bytes_accessed=8 << 20, transcendentals=1 << 20),
    )(core, total, part_m, part_p, bias, cosines, sines, back, places, send_rows)


def multiply_kernel(sizes, w_ref, *refs):
    at = 0
    outs = refs[sum(sizes) :]
    for count, out_ref in zip(sizes, outs):
        total, depth = 0.0, 0
        for ref in refs[at : at + count]:
            total += jnp.dot(
                ref[...], w_ref[depth : depth + ref.shape[1]], preferred_element_type=F32
            )
            depth += ref.shape[1]
        out_ref[...] = total
        at += count


def multiply(products, w):
    flat = [t for pieces in products for t in pieces]
    vmem = pl.BlockSpec(memory_space=pltpu.VMEM)
    return pl.pallas_call(
        functools.partial(multiply_kernel, [len(pieces) for pieces in products]),
        out_shape=[jax.ShapeDtypeStruct((p[0].shape[0], w.shape[1]), F32) for p in products],
        in_specs=[vmem] * (1 + len(flat)),
        out_specs=[vmem] * len(products),
        compiler_params=pltpu.CompilerParams(vmem_limit_bytes=32 * 1024 * 1024),
        cost_estimate=pl.CostEstimate(flops=1 << 20, bytes_accessed=1 << 12, transcendentals=0),
    )(w, *flat)


def project_out_kernel(mine_ref, theirs_ref, w_ref, out_ref):
    both = jnp.concatenate([mine_ref[...], theirs_ref[...]], axis=1)
    w = jnp.concatenate([w_ref[i] for i in range(w_ref.shape[0])], axis=1)
    out_ref[...] = jnp.dot(both, w, preferred_element_type=F32).astype(BF)


def project_out(first, count, mine, theirs, w):
    rows, depth = mine.shape
    _, deep, width = w.shape
    group = 2
    whole = pl.BlockSpec((rows, depth), lambda d: (0, 0))
    return pl.pallas_call(
        project_out_kernel,
        out_shape=jax.ShapeDtypeStruct((rows, count * width), BF),
        grid=(count // group,),
        in_specs=[whole, whole, pl.BlockSpec((group, deep, width), lambda d: (first // group + d, 0, 0))],
        out_specs=pl.BlockSpec((rows, group * width), lambda d: (0, d)),
        compiler_params=pltpu.CompilerParams(vmem_limit_bytes=48 * 1024 * 1024),
        cost_estimate=pl.CostEstimate(
            flops=2 * rows * deep * width * count, bytes_accessed=8 << 20, transcendentals=0
        ),
    )(mine, theirs, w)


def interleave_kernel(side, width, at_ref, *refs):
    *parts, out_ref = refs
    core, y = at_ref[0], at_ref[1]
    first = 0
    for j in range(len(parts) // 2):
        blocks = parts[2 * j].shape[1] // width
        first += parts[2 * j - 2].shape[1] // width if j else 0
        for i in range(blocks):
            z, back = divmod(first + i, side)
            at = lax.rem(y + side - back, side) * side + z
            for part, c in ((parts[2 * j], core), (parts[2 * j + 1], 1 - core)):
                to = pl.multiple_of((at * 2 + c) * width, width)
                out_ref[:, pl.ds(to, width)] = part[:, i * width : (i + 1) * width]


def interleave(side, width, at, parts):
    rows, cols = parts[0].shape[0], sum(p.shape[1] for p in parts)
    vmem = pl.BlockSpec(memory_space=pltpu.VMEM)
    return pl.pallas_call(
        functools.partial(interleave_kernel, side, width),
        out_shape=jax.ShapeDtypeStruct((rows, cols), BF),
        in_specs=[pl.BlockSpec(memory_space=pltpu.SMEM)] + [vmem] * len(parts),
        out_specs=vmem,
    )(at, *parts)


def shards(
    hidden_in,
    norm_gain,
    query_weight,
    keyval_weight,
    query_bias,
    keyval_bias,
    out_weight,
    lengths,
    move_plan,
    first_len,
):
    packs = lax.axis_size(DP)
    pack = lax.axis_index(DP)
    x = lax.axis_index("x")
    y = lax.axis_index("y")
    core = lax.axis_index("c")
    nx = lax.axis_size("x")
    ny = lax.axis_size("y")
    z = lax.axis_index("z")
    nz = lax.axis_size("z")
    here = hidden_in.shape[0]
    width = hidden_in.shape[1]
    rows = here * nx * 2
    q_cols = query_weight.shape[1]

    r = jnp.arange(here, dtype=jnp.int32)
    places = jnp.concatenate(
        [
            here * (2 * ((x - s) % nx) + (core if k == 0 else 1 - core)) + r
            for k in range(2)
            for s in range(4)
        ]
    )
    places_out = jnp.concatenate(
        [here * (2 * ((x - s) % nx) + k) + r for s in range(4) for k in range(2)]
    )

    ids = jnp.arange(lengths.shape[0], dtype=jnp.int32)
    offsets = jnp.cumsum(lengths) - lengths
    bundle = jnp.sum((places[:, None] >= offsets[None, :]).astype(jnp.int32), axis=1) - 1
    selector = (bundle[:, None] == ids[None, :]).astype(jnp.int32)
    starts = jnp.sum(selector * offsets[None, :], axis=1)
    first_here = jnp.sum(first_len * (jnp.arange(packs)[:, None] == pack).astype(jnp.int32), axis=0)
    splits = jnp.sum(selector * first_here[None, :], axis=1)
    back = places - starts
    back = back - jnp.where(back >= splits, splits, 0)
    indices = jnp.arange(HD // 2, dtype=F32)
    angles = back.astype(F32)[:, None] * (THETA ** (-2.0 * indices / HD))[None, :]
    cosines, sines = jnp.cos(angles), jnp.sin(angles)
    cosines = jnp.concatenate([cosines, cosines], axis=1)
    sines = jnp.concatenate([-sines, sines], axis=1)

    combined = jnp.concatenate([query_weight, keyval_weight.reshape(keyval_weight.shape[0], -1)], axis=1)
    hidden_in, combined = after(hidden_in, combined)
    w_in = lax.all_gather(combined, "z", axis=0, tiled=True)
    block = width // ny
    half = block // 2

    values = hidden_in.astype(F32)
    scale = lax.rsqrt(jnp.mean(values * values, axis=1, keepdims=True) + EPS)
    own = (values * scale * norm_gain).astype(BF)

    def features(step):
        return lax.dynamic_slice_in_dim(own, (y + step) % ny * block, block, axis=1)

    pack_0 = features(0)
    with jax.named_scope("exchange"):
        rest = jnp.concatenate(
            [hop(features(2), "y", 2), hop(features(1), "y", 1), hop(features(-1), "y", -1)], axis=0
        )

    cols = out_weight.shape[1] // 2
    w_low, w_high = out_weight[:, :cols], out_weight[:, cols:]
    mine = jnp.where(core == 0, w_low, w_high)
    other = swap(jnp.where(core == 0, w_high, w_low))
    with jax.named_scope("own"):
        left_0, right_0 = hop(pack_0, "x", 1), hop(pack_0, "x", -1)
        low_0, high_0 = hop(left_0[:, :half], "x", 1), hop(right_0[:, half:], "x", -1)
    w_both = jnp.concatenate([mine, other], axis=0)
    rest, left_0, right_0, low_0, high_0, cosines, sines, w_both = after(
        rest, left_0, right_0, low_0, high_0, cosines, sines, w_both
    )

    rest_other = swap(rest)
    with jax.named_scope("w_out"):
        w_near = jnp.stack([w_both, hop(w_both, "y", 1), hop(w_both, "y", 2), hop(w_both, "y", 3)])

    with jax.named_scope("rest"):
        left, right = hop(rest, "x", 1), hop(rest, "x", -1)
        low, high = hop(left[:, :half], "x", 1), hop(right[:, half:], "x", -1)
    w_near, left, right = after(w_near, left, right)
    w_out = lax.all_gather(w_near, "z", axis=0, tiled=True)

    with jax.named_scope("rest"):
        near = [rest, left, right]
        near_sums = [multiply([[t] for t in side], w_in) for side in (near, [rest_other, swap(left), swap(right)])]
        (low, high), near_sums, mine = after(
            (low, high), near_sums, (pack_0, left_0, low_0, high_0, right_0)
        )
        far_sums = [multiply([side], w_in) for side in ([low, high], [swap(low), swap(high)])]
    with jax.named_scope("own"):
        mine = jnp.concatenate(
            [mine[0], mine[1], jnp.concatenate(mine[2:4], axis=1), mine[4]], axis=0
        )
        sum_0 = jnp.concatenate([dot(mine, w_in), dot(swap(mine), w_in)], axis=0)

    def whole(i):
        at = slice(i * here, (i + 1) * here)
        return jnp.concatenate(
            [t[at] for n, f in zip(near_sums, far_sums) for t in (n[0], n[1], f[0], n[2])], axis=0
        )

    sum_2, sum_m, sum_p = whole(0), whole(1), whole(2)

    mid = sum_0.shape[1] // 2
    two = sum_2.astype(BF)
    a = hop(two[:, :mid], "y", 1)
    b = hop(two[:, mid:], "y", -1)
    up = jnp.concatenate(
        [(sum_p[:, :mid] + a.astype(F32)).astype(BF), sum_p[:, mid:].astype(BF)], axis=1
    )
    down = jnp.concatenate(
        [sum_m[:, :mid].astype(BF), (sum_m[:, mid:] + b.astype(F32)).astype(BF)], axis=1
    )
    from_m = hop(up, "y", 1)
    from_p = hop(down, "y", -1)

    capacity = 2 * rows // packs
    lanes = jnp.arange(capacity, dtype=jnp.int32)
    slots = jnp.arange(packs, dtype=jnp.int32)
    outgoing = (move_plan[None, :] == ((slots - pack) % packs)[:, None]).astype(jnp.int32)
    send_start = jnp.sum(outgoing * offsets[None, :], axis=1)
    send_length = jnp.sum(outgoing * lengths[None, :], axis=1)
    live = lanes[None, :] < send_length[:, None]
    send_rows = jnp.where(live, send_start[:, None] + lanes[None, :], -1).reshape(-1)
    bias = jnp.concatenate([query_bias, keyval_bias.reshape(-1)])[None, :]
    sent = attend(
        here,
        q_cols // HD,
        packs * capacity,
        core.reshape(1),
        sum_0,
        from_m,
        from_p,
        bias,
        cosines,
        sines,
        back[:, None],
        places[None, :],
        send_rows[:, None],
    ).reshape(packs, capacity, q_cols)
    got = lax.all_to_all(sent, DP, split_axis=0, concat_axis=0, tiled=True)
    sources = (pack - move_plan) % packs
    bundle_out = jnp.sum((places_out[:, None] >= offsets[None, :]).astype(jnp.int32), axis=1) - 1
    selector = (bundle_out[:, None] == ids[None, :]).astype(jnp.int32)
    source = jnp.sum(selector * sources[None, :], axis=1)
    slot = source * capacity + places_out - jnp.sum(selector * offsets[None, :], axis=1)
    place = (slot[:, None] == jnp.arange(packs * capacity, dtype=jnp.int32)[None, :]).astype(BF)
    moved = dot(place, got.reshape(packs * capacity, q_cols)).astype(BF)
    theirs = swap(moved)

    parts = []
    pair = 2 * here
    short = packs // 4
    for first, count in ((0, short), (short, packs - short)):
        partial = project_out(first, count, moved, theirs, w_out)
        part = [partial[s * pair : (s + 1) * pair] for s in range(4)]
        mid = part[0].shape[1] // 2
        a = hop(part[2][:, :mid], "x", 1)
        b = hop(part[2][:, mid:], "x", -1)
        up = jnp.concatenate(
            [(part[3][:, :mid].astype(F32) + a.astype(F32)).astype(BF), part[3][:, mid:]], axis=1
        )
        down = jnp.concatenate(
            [part[1][:, :mid], (part[1][:, mid:].astype(F32) + b.astype(F32)).astype(BF)], axis=1
        )
        u, v = hop(up, "x", 1), hop(down, "x", -1)
        total = (part[0].astype(F32) + u.astype(F32) + v.astype(F32)).astype(BF)
        parts.append(jnp.where(core == 0, total[:here], total[here:]))
        parts.append(swap(jnp.where(core == 0, total[here:], total[:here])))
    return interleave(ny, cols, jnp.stack([core, y]), parts)


def solution(mesh):
    packs, tensor = mesh.devices.shape
    side = int(round(packs**0.5))
    fine = Mesh(mesh.devices.reshape(side, packs // side, tensor // 2, 2), ("y", "z", "x", "c"))
    every = ("y", "z", "x", "c")
    heads = ("x", "c")
    in_specs = (
        P(every, None),
        P(),
        P(DP, heads),
        P(DP, None, heads),
        P(heads),
        P(None, heads),
        P(heads, DP),
        P(),
        P(),
        P(),
    )
    return jax.shard_map(
        shards, mesh=fine, in_specs=in_specs, out_specs=P(every, None), check_vma=False
    )
```
